256 devices in a mesh: dp: 32 (over z, x), fsdp: 2 (over core), tensor: 4 (over y).
Axes of the slice: x: 4, y: 4, z: 8, core: 2. Of those that a mesh axis runs over, the one named last changes fastest.
Arguments:
- activations: bfloat16 [1, 16384, 8192], P(None, ('dp', 'tensor'), 'fsdp'), may hold values from -6 to 6
- cotangents: bfloat16 [1, 16384, 28672], P(None, ('dp', 'fsdp'), 'tensor'), may hold values from -16 to 16
- projector: bfloat16 [8192, 1024], P('fsdp'), may hold values from -0.0625 to 0.0625
- first_moment: float32 [1, 4, 7168, 1024], P(None, 'tensor', 'dp', 'fsdp'), may hold values from -60 to 60
- second_moment: float32 [1, 4, 7168, 1024], P(None, 'tensor', 'dp', 'fsdp'), may hold values from 1 to 16
Outputs:
- update: float32 [1, 4, 7168, 8192], P(None, 'tensor', 'dp', 'fsdp')
- new_first: float32 [1, 4, 7168, 1024], P(None, 'tensor', 'dp', 'fsdp')
- new_second: float32 [1, 4, 7168, 1024], P(None, 'tensor', 'dp', 'fsdp')
The draws below stay inside these ranges and needn't reach their ends.
All inputs are finite; a program needn't handle non-finite values.
Results may differ from the reference program's by a relative error of at most 0.029.
Values may be sent and summed in bfloat16 or wider, within the bound.
A program may use at most 128 MiB of HBM per device.

```python
import math
import jax
import jax.numpy as jnp
from jax import lax

D = 8192
FF = 28672
RANK = 1024
LAYERS = 1
REP_TOK = 512
FFT = 7168
TOKENS = 16384
N_DP = 32


def with_spikes(values, key, source, target, blocks, factor):
    owner, partner = [(jnp.arange(values.shape[position]) // (values.shape[position] // blocks)).reshape([-1 if axis == position else 1 for axis in range(values.ndim)]) for position in (source, target)]
    chosen = jax.random.permutation(key, blocks)[partner]
    strong = (owner == chosen) | (owner == (partner + blocks // 2) % blocks)
    return jnp.where(strong, factor * values, values)


def levels(key, dims, shards, least, largest):
    level = 1.0
    for dim, shards_of in shards:
        steps = jax.random.uniform(jax.random.fold_in(jax.random.fold_in(key, 6), dim), (shards_of,), jnp.float32, least / len(shards), largest / len(shards))
        level = level * jnp.repeat(jnp.exp(steps), dims[dim] // shards_of).reshape((-1,) + (1,) * (len(dims) - 1 - dim))
    return level


def bell_draw(key, extent, width, bound, shards=(), kind=jnp.bfloat16):
    gain = levels(key, extent, shards, -0.22, 0.18) if shards else 1.0
    values = jax.random.normal(key, extent, jnp.float32) * width * gain
    return jnp.minimum(jnp.maximum(values, -bound), bound).astype(kind)


def noise_with(own_key, dims, scale, most, split, heavy, held_as=jnp.bfloat16):
    result = scale * jax.random.normal(own_key, dims, jnp.float32)
    if split:
        result = result * levels(own_key, dims, split, -0.22, 0.18)
    return jnp.clip(with_spikes(result, jax.random.fold_in(own_key, 3), *heavy), -most, most).astype(held_as)


def setup_inputs(seed: int = 0) -> dict:
    streams_of = jax.random.split(jax.random.key(seed), 6)
    activations = bell_draw(streams_of[0], (LAYERS, TOKENS, D), 1.0, 6.0, ((1, 128), (2, 2)))
    cotangents = noise_with(streams_of[1], (LAYERS, TOKENS, FF), 1.0, 16.0, ((1, 64), (2, 4)), (1, 2, 64, 4.0))
    projector = bell_draw(streams_of[2], (D, RANK), D ** -0.5, 0.0625, ((0, 2),))
    first_moment = bell_draw(streams_of[3], (LAYERS, FF // FFT, FFT, RANK), 10.0, 60.0, ((1, 4), (2, 32), (3, 2)), jnp.float32)
    second_moment = jnp.clip(jnp.exp(math.log(16.0) - 2.7725887 * jax.random.uniform(streams_of[4], (LAYERS, FF // FFT, FFT, RANK), jnp.float32) ** levels(streams_of[4], (LAYERS, FF // FFT, FFT, RANK), ((1, 4), (2, 32), (3, 2)), -0.2, 0.2)), 1.0, 16.0)
    return {"activations": activations, "cotangents": cotangents, "projector": projector, "first_moment": first_moment, "second_moment": second_moment}


beta_first = 0.9
beta_second = 0.999
bias_first = 1.0 - 0.9 ** 10
bias_second = 1.0 - 0.999 ** 10
adam_eps = 1e-08

def reference(activations, cotangents, projector, first_moment, second_moment):
    updates = []
    firsts = []
    seconds = []
    for layer_idx in range(LAYERS):
        projected = jnp.dot(activations[layer_idx], projector, preferred_element_type=jnp.float32).astype(jnp.bfloat16)
        grads = cotangents[layer_idx]

        def add_group(running, group):
            offset = (group * REP_TOK).astype(jnp.int32)
            rows_grad = lax.dynamic_slice_in_dim(grads, offset, REP_TOK, 0)
            rows_proj = lax.dynamic_slice_in_dim(projected, offset, REP_TOK, 0)
            term = jnp.dot(rows_grad.T, rows_proj, preferred_element_type=jnp.float32)
            rounded = lax.optimization_barrier(term.astype(jnp.bfloat16))
            return (running + rounded.astype(jnp.float32), None)
        lowrank, _ = lax.scan(add_group, jnp.zeros((FF, RANK), jnp.float32), jnp.arange(N_DP, dtype=jnp.int32))
        moment = first_moment[layer_idx].reshape(FF, RANK)
        second = second_moment[layer_idx].reshape(FF, RANK)
        fresh_first = beta_first * moment + (1.0 - beta_first) * lowrank
        fresh_second = beta_second * second + (1.0 - beta_second) * lowrank * lowrank
        direction = (fresh_first / bias_first / (jnp.sqrt(fresh_second / bias_second) + adam_eps)).astype(jnp.bfloat16)
        blocks = direction.reshape(FF // FFT, FFT, RANK)
        update = lax.map(lambda block_rows: jnp.dot(block_rows, projector.T, preferred_element_type=jnp.float32), blocks)
        updates.append(update)
        firsts.append(fresh_first.reshape(FF // FFT, FFT, RANK))
        seconds.append(fresh_second.reshape(FF // FFT, FFT, RANK))
    return (jnp.stack(updates), jnp.stack(firsts), jnp.stack(seconds))
```

```python
import functools

import jax
import jax.numpy as jnp
from jax import lax
from jax.experimental import pallas as pl
from jax.experimental.pallas import tpu as pltpu
from jax.sharding import PartitionSpec as P

beta_first = 0.9
beta_second = 0.999
bias_first = 1.0 - 0.9**10
bias_second = 1.0 - 0.999**10
adam_eps = 1e-08

NZ, NX, NY = 8, 4, 4
TOK = 128
WIDTH = 4096
RANK = 1024
HALF = 512
ROWS = 224
UNIT = NX * ROWS
HID = NZ * UNIT
RX = 128
RZ = ROWS - RX
QUARTER = HALF // 2
KCH = 4
F32, BF16 = jnp.float32, jnp.bfloat16
MESH = pl.DeviceIdType.MESH

STEPS = (4, 3, -3, 2, -2, 1, -1, 0)


def dot(a, b, dims):
    return lax.dot_general(a, b, (dims, ((), ())), preferred_element_type=F32)


def kernel(
    act, cot, projector, first, second, upd, new_first, new_second,
    act_v, prj_v, cot_v, part_v, other_v, proj_v, term, xr, zz, zx, xz, dir_v, first_v, second_v,
    load, cot_load, cot_s, cot_r, part_s, part_r, y_s, y_r, xr_s, xr_r, zz_s, zz_r,
    zx_s, zx_r, xz_s, xz_r, dir_s, dir_r,
):
    dp, core, y = lax.axis_index("dp"), lax.axis_index("fsdp"), lax.axis_index("tensor")
    z, x = dp // NX, dp % NX

    def at_x(k):
        return (z * NX + (x + k + NX) % NX, core, y)

    def at_z(k):
        return (((z + k + NZ) % NZ) * NX + x, core, y)

    def at_y(k):
        return (dp, core, (y + k) % NY)

    sibling = (dp, 1 - core, y)

    def remote(src, dst, send, recv, device):
        return pltpu.make_async_remote_copy(
            src_ref=src, dst_ref=dst, send_sem=send, recv_sem=recv, device_id=device, device_id_type=MESH
        )

    def unit_cols(i):
        return pl.ds(pl.multiple_of(((z + STEPS[i] + NZ) % NZ) * UNIT, UNIT), UNIT)

    own_tok = pl.ds(pl.multiple_of(core * 256, 256), 256)
    loads = [pltpu.make_async_copy(act.at[0], act_v, load.at[0])]
    kk = WIDTH // KCH
    for c in range(KCH):
        rows = pl.ds(c * kk, kk)
        loads.append(pltpu.make_async_copy(projector.at[rows], prj_v.at[rows], load.at[1 + c]))
    loads.append(pltpu.make_async_copy(first.at[0, 0], first_v, load.at[1 + KCH]))
    loads.append(pltpu.make_async_copy(second.at[0, 0], second_v, load.at[2 + KCH]))
    for c in loads[: 1 + KCH]:
        c.start()
    cot_in = [
        pltpu.make_async_copy(cot.at[0, :, unit_cols(i)], cot_v.at[own_tok, unit_cols(i)], cot_load.at[i])
        for i in range(NZ)
    ]
    for c in cot_in:
        c.start()
    for c in loads[1 + KCH :]:
        c.start()

    barrier = pltpu.get_barrier_semaphore()
    for device in (sibling, at_y(1), at_y(2), at_y(3), at_x(1), at_x(-1), at_z(1), at_z(-1)):
        pl.semaphore_signal(barrier, inc=1, device_id=device, device_id_type=MESH)
    pl.semaphore_wait(barrier, 8)

    cot_x = [
        remote(cot.at[0, :, unit_cols(i)], cot_v.at[own_tok, unit_cols(i)], cot_s.at[i], cot_r.at[i], sibling)
        for i in range(NZ)
    ]
    for c in cot_x[:2]:
        c.start()

    loads[0].wait()
    for c in range(KCH):
        loads[1 + c].wait()
        piece = dot(act_v[:, c * kk : (c + 1) * kk], prj_v[c * kk : (c + 1) * kk, :], ((1,), (0,)))
        for h in range(2):
            block = piece[:, h * HALF : (h + 1) * HALF]
            if c == 0:
                part_v[h] = block
            else:
                part_v[h] += block
    swap = remote(part_v.at[1 - core], other_v, part_s.at[0], part_r.at[0], sibling)
    swap.start()
    for c in cot_x[2:]:
        c.start()
    swap.wait_recv()
    own_rows = pl.ds(pl.multiple_of(y * TOK, TOK), TOK)
    proj_v[own_rows, :] = (part_v[core] + other_v[...]).astype(BF16)
    gather = [
        remote(proj_v.at[own_rows], proj_v.at[own_rows], y_s.at[k - 1], y_r.at[k - 1], at_y(k)) for k in (2, 1, 3)
    ]
    for c in gather:
        c.start()
    for c in gather:
        c.wait_recv()

    def place(i, j, first_row, rows):
        base = ((z + STEPS[i] + NZ) % NZ) * UNIT + ((x + j + NX) % NX) * ROWS + first_row
        return pl.ds(pl.multiple_of(base, 32), rows)

    def x_rows(i, j):
        return place(i, j, 0, RX)

    def z_rows(i, j):
        return place(i, j, RX, RZ)

    def compute(i):
        cot_in[i].wait()
        cot_x[i].wait_recv()
        term[unit_cols(i), :] = dot(cot_v[:, unit_cols(i)], proj_v[...], ((0,), (0,))).astype(BF16)

    sends = list(cot_x) + [swap] + gather

    def start(copy):
        copy.start()
        sends.append(copy)
        return copy

    x_first = {}

    def x_open(i):
        s = 1 - 2 * (i % 2)
        x_first[i, 0] = start(
            remote(term.at[x_rows(i, 2 * s)], xr.at[i, 0], xr_s.at[i, 0], xr_r.at[i, 0], at_x(s))
        )
        x_first[i, 2] = start(
            remote(term.at[x_rows(i, -s)], xr.at[i, 2], xr_s.at[i, 2], xr_r.at[i, 2], at_x(-s))
        )

    def x_forward(i):
        s = 1 - 2 * (i % 2)
        x_first[i, 0].wait_recv()
        rows = x_rows(i, s)
        term[rows, :] = term[rows, :] + xr[i, 0]
        x_first[i, 1] = start(remote(term.at[rows], xr.at[i, 1], xr_s.at[i, 1], xr_r.at[i, 1], at_x(s)))

    zx_copies = {}

    def x_close(i):
        x_first[i, 1].wait_recv()
        x_first[i, 2].wait_recv()
        rows = x_rows(i, 0)
        total = term[rows, :].astype(F32) + xr[i, 1].astype(F32) + xr[i, 2].astype(F32)
        if i == 0:
            term[rows, :] = total.astype(BF16)
            for n, (s, lanes) in enumerate(((1, pl.ds(0, QUARTER)), (-1, pl.ds(QUARTER, QUARTER)))):
                zx_copies[0, s] = start(
                    remote(term.at[rows, lanes], zx.at[0, :, lanes], zx_s.at[7 * n], zx_r.at[7 * n], at_z(s))
                )
            return None
        if i == 7:
            zx_copies[5].wait_recv()
            zx_copies[6].wait_recv()
            return total + zx[5].astype(F32) + zx[6].astype(F32)
        s = 1 if STEPS[i] > 0 else -1
        if i in (1, 2):
            lanes = slice(0, QUARTER) if s == 1 else slice(QUARTER, HALF)
            rest = slice(QUARTER, HALF) if s == 1 else slice(0, QUARTER)
            zx_copies[0, s].wait_recv()
            term[rows, lanes] = (total[:, lanes] + zx[0, :, lanes].astype(F32)).astype(BF16)
            term[rows, rest] = total[:, rest].astype(BF16)
        else:
            zx_copies[i - 2].wait_recv()
            term[rows, :] = (total + zx[i - 2].astype(F32)).astype(BF16)
        zx_copies[i] = start(remote(term.at[rows], zx.at[i], zx_s.at[i], zx_r.at[i], at_z(s)))
        return None

    zz_copies = {}

    def z_step(i):
        s = 1 if STEPS[i] > 0 else -1
        for j in range(NX):
            rows = z_rows(i, j)
            if i == 0:
                s = 1 if j < 2 else -1
            elif i in (1, 2):
                if (j < 2) == (s == 1):
                    zz_copies[0, j].wait_recv()
                    term[rows, :] = term[rows, :] + zz[0, j]
            elif i < 7:
                zz_copies[i - 2, j].wait_recv()
                term[rows, :] = term[rows, :] + zz[i - 2, j]
            zz_copies[i, j] = start(
                remote(term.at[rows], zz.at[i, j], zz_s.at[i, j], zz_r.at[i, j], at_z(s))
            )

    def z_total(j):
        zz_copies[5, j].wait_recv()
        zz_copies[6, j].wait_recv()
        return term[z_rows(7, j), :].astype(F32) + zz[5, j].astype(F32) + zz[6, j].astype(F32)

    xz_copies = {}

    def z_open():
        rows = z_rows(7, 2)
        term[rows, :] = z_total(2).astype(BF16)
        for n, (s, lanes) in enumerate(((1, pl.ds(0, QUARTER)), (-1, pl.ds(QUARTER, QUARTER)))):
            xz_copies[0, s] = start(
                remote(term.at[rows, lanes], xz.at[0, :, lanes], xz_s.at[3 * n], xz_r.at[3 * n], at_x(s))
            )

    def z_forward(n):
        s = 1 if n == 1 else -1
        j = s % NX
        total = z_total(j)
        lanes = slice(0, QUARTER) if s == 1 else slice(QUARTER, HALF)
        rest = slice(QUARTER, HALF) if s == 1 else slice(0, QUARTER)
        rows = z_rows(7, j)
        xz_copies[0, s].wait_recv()
        term[rows, lanes] = (total[:, lanes] + xz[0, :, lanes].astype(F32)).astype(BF16)
        term[rows, rest] = total[:, rest].astype(BF16)
        xz_copies[n] = start(remote(term.at[rows], xz.at[n], xz_s.at[n], xz_r.at[n], at_x(s)))

    def z_close():
        total = z_total(0)
        xz_copies[1].wait_recv()
        xz_copies[2].wait_recv()
        return total + xz[1].astype(F32) + xz[2].astype(F32)

    dir_copies = []
    own_lanes = pl.ds(pl.multiple_of(core * HALF, HALF), HALF)

    def adam(lowrank, rows):
        fresh_first = beta_first * first_v[rows, :] + (1.0 - beta_first) * lowrank
        fresh_second = beta_second * second_v[rows, :] + (1.0 - beta_second) * lowrank * lowrank
        new_first[0, 0, rows, :] = fresh_first
        new_second[0, 0, rows, :] = fresh_second
        direction = fresh_first / bias_first / (jnp.sqrt(fresh_second / bias_second) + adam_eps)
        dir_v[rows, own_lanes] = direction.astype(BF16)
        n = len(dir_copies)
        dir_copies.append(
            start(
                remote(dir_v.at[rows, own_lanes], dir_v.at[rows, own_lanes], dir_s.at[n], dir_r.at[n], sibling)
            )
        )

    def back_project(n, rows):
        dir_copies[n].wait_recv()
        left = dir_v[rows, :]
        for c in range(8):
            cols = slice(c * 512, (c + 1) * 512)
            upd[0, 0, rows, cols] = dot(left, prj_v[cols, :], ((1,), (1,)))

    compute(0), x_open(0), z_step(0)
    compute(1), x_open(1), z_step(1)
    compute(2), x_open(2), z_step(2)
    compute(3), x_open(3), x_forward(0)
    compute(4), x_open(4), x_forward(1)
    z_step(3), z_step(4), x_close(0)
    compute(5), x_open(5), x_forward(2)
    compute(6), x_open(6), x_close(1)
    compute(7), x_open(7), x_forward(3)
    x_close(2), x_forward(4)
    z_step(5), z_step(6)
    x_close(3), x_forward(5)
    x_close(4), x_forward(6)
    x_close(5), x_forward(7)
    z_open(), x_close(6)
    z_forward(1), z_forward(2)
    for c in loads[1 + KCH :]:
        c.wait()
    z_rows_own, x_rows_own = pl.ds(RX, RZ), pl.ds(0, RX)
    adam(z_close(), z_rows_own)
    back_project(0, z_rows_own)
    adam(x_close(7), x_rows_own)
    back_project(1, x_rows_own)
    for c in sends:
        c.wait_send()


def per_device(activations, cotangents, projector, first_moment, second_moment):
    any_space = pl.BlockSpec(memory_space=pl.ANY)
    vmem = pl.BlockSpec(memory_space=pltpu.VMEM)
    dma = pltpu.SemaphoreType.DMA
    return pl.pallas_call(
        kernel,
        out_shape=(
            jax.ShapeDtypeStruct((1, 1, ROWS, WIDTH), F32),
            jax.ShapeDtypeStruct((1, 1, ROWS, HALF), F32),
            jax.ShapeDtypeStruct((1, 1, ROWS, HALF), F32),
        ),
        in_specs=[any_space] * 5,
        out_specs=(vmem, vmem, vmem),
        scratch_shapes=[
            pltpu.VMEM((TOK, WIDTH), BF16),
            pltpu.VMEM((WIDTH, RANK), BF16),
            pltpu.VMEM((512, HID), BF16),
            pltpu.VMEM((2, TOK, HALF), F32),
            pltpu.VMEM((TOK, HALF), F32),
            pltpu.VMEM((512, HALF), BF16),
            pltpu.VMEM((HID, HALF), BF16),
            pltpu.VMEM((8, 3, RX, HALF), BF16),
            pltpu.VMEM((7, NX, RZ, HALF), BF16),
            pltpu.VMEM((7, RX, HALF), BF16),
            pltpu.VMEM((3, RZ, HALF), BF16),
            pltpu.VMEM((ROWS, RANK), BF16),
            pltpu.VMEM((ROWS, HALF), F32),
            pltpu.VMEM((ROWS, HALF), F32),
            dma((3 + KCH,)),
            dma((8,)),
            dma((8,)),
            dma((8,)),
            dma((1,)),
            dma((1,)),
            dma((3,)),
            dma((3,)),
            dma((8, 3)),
            dma((8, 3)),
            dma((7, NX)),
            dma((7, NX)),
            dma((8,)),
            dma((8,)),
            dma((4,)),
            dma((4,)),
            dma((2,)),
            dma((2,)),
        ],
        compiler_params=pltpu.CompilerParams(
            collective_id=0, has_side_effects=True, vmem_limit_bytes=56 * 2**20
        ),
        name="galore_step",
    )(activations, cotangents, projector, first_moment, second_moment)


def solution(mesh):
    return jax.shard_map(
        per_device,
        mesh=mesh,
        in_specs=(
            P(None, ("dp", "tensor"), "fsdp"),
            P(None, ("dp", "fsdp"), "tensor"),
            P("fsdp", None),
            P(None, "tensor", "dp", "fsdp"),
            P(None, "tensor", "dp", "fsdp"),
        ),
        out_specs=(
            P(None, "tensor", "dp", "fsdp"),
            P(None, "tensor", "dp", "fsdp"),
            P(None, "tensor", "dp", "fsdp"),
        ),
        check_vma=False,
    )
```

```python
import functools

import jax
import jax.numpy as jnp
from jax import lax
from jax.experimental import pallas as pl
from jax.experimental.pallas import tpu as pltpu
from jax.sharding import PartitionSpec as P

beta_first = 0.9
beta_second = 0.999
bias_first = 1.0 - 0.9**10
bias_second = 1.0 - 0.999**10
adam_eps = 1e-08

NZ, NX, NY = 8, 4, 4
TOK = 128
WIDTH = 4096
RANK = 1024
HALF = 512
ROWS = 224
UNIT = NX * ROWS
HID = NZ * UNIT
RX = 128
RZ = ROWS - RX
QUARTER = HALF // 2
KCH = 4
COLS = 512
F32, BF16 = jnp.float32, jnp.bfloat16
MESH = pl.DeviceIdType.MESH

STEPS = (4, 3, -3, 2, -2, 1, -1, 0)

ORDER = (
    "C0", "X0", "Z02", "Z01", "C1", "Z12", "X1", "Z13", "C2", "X2", "Z21", "Z00", "Z20", "C3",
    "X3", "C4", "C5", "F0", "Z11", "Z22", "X4", "Z03", "X5", "C6", "Z41", "Z32", "C7", "F1",
    "X7", "Z33", "Z40", "X6", "F2", "Z42", "Z10", "Z23", "Z31", "F3", "Z61", "Z52", "L0", "Z60",
    "Z53", "F4", "Z30", "Z62", "F5", "Z43", "Z51", "F7", "L1", "F6", "O", "Z50", "L2", "Z63",
    "L3", "L4", "G1", "G2", "L5", "L6",
)


def dot(a, b, dims):
    return lax.dot_general(a, b, (dims, ((), ())), preferred_element_type=F32)


def kernel(
    act, cot, projector, first, second, dir_v, new_first, new_second,
    act_v, prj_v, cot_v, part_v, other_v, proj_v, term, xr, zz, zx, xz, first_v, second_v,
    load, cot_load, cot_s, cot_r, part_s, part_r, y_s, y_r, xr_s, xr_r, zz_s, zz_r,
    zx_s, zx_r, xz_s, xz_r, dir_s, dir_r,
):
    dp, core, y = lax.axis_index("dp"), lax.axis_index("fsdp"), lax.axis_index("tensor")
    z, x = dp // NX, dp % NX

    def at_x(k):
        return (z * NX + (x + k + NX) % NX, core, y)

    def at_z(k):
        return (((z + k + NZ) % NZ) * NX + x, core, y)

    def at_y(k):
        return (dp, core, (y + k) % NY)

    sibling = (dp, 1 - core, y)

    def remote(src, dst, send, recv, device):
        return pltpu.make_async_remote_copy(
            src_ref=src, dst_ref=dst, send_sem=send, recv_sem=recv, device_id=device, device_id_type=MESH
        )

    def unit_cols(i):
        return pl.ds(pl.multiple_of(((z + STEPS[i] + NZ) % NZ) * UNIT, UNIT), UNIT)

    own_tok = pl.ds(pl.multiple_of(core * 256, 256), 256)
    loads = [pltpu.make_async_copy(act.at[0], act_v, load.at[0])]
    kk = WIDTH // KCH
    for c in range(KCH):
        rows = pl.ds(c * kk, kk)
        loads.append(pltpu.make_async_copy(projector.at[rows], prj_v.at[rows], load.at[1 + c]))
    loads.append(pltpu.make_async_copy(first.at[0, 0], first_v, load.at[1 + KCH]))
    loads.append(pltpu.make_async_copy(second.at[0, 0], second_v, load.at[2 + KCH]))
    for c in loads[: 1 + KCH]:
        c.start()
    cot_in = [
        pltpu.make_async_copy(cot.at[0, :, unit_cols(i)], cot_v.at[own_tok, unit_cols(i)], cot_load.at[i])
        for i in range(NZ)
    ]
    for c in cot_in:
        c.start()
    for c in loads[1 + KCH :]:
        c.start()

    barrier = pltpu.get_barrier_semaphore()
    for device in (sibling, at_y(1), at_y(2), at_y(3), at_x(1), at_x(-1), at_z(1), at_z(-1)):
        pl.semaphore_signal(barrier, inc=1, device_id=device, device_id_type=MESH)
    pl.semaphore_wait(barrier, 8)

    cot_x = [
        remote(cot.at[0, :, unit_cols(i)], cot_v.at[own_tok, unit_cols(i)], cot_s.at[i], cot_r.at[i], sibling)
        for i in range(NZ)
    ]
    for c in cot_x[:2]:
        c.start()

    loads[0].wait()
    for c in range(KCH):
        loads[1 + c].wait()
        piece = dot(act_v[:, c * kk : (c + 1) * kk], prj_v[c * kk : (c + 1) * kk, :], ((1,), (0,)))
        for h in range(2):
            block = piece[:, h * HALF : (h + 1) * HALF]
            if c == 0:
                part_v[h] = block
            else:
                part_v[h] += block
    swap = remote(part_v.at[1 - core], other_v, part_s.at[0], part_r.at[0], sibling)
    swap.start()
    for c in cot_x[2:]:
        c.start()
    swap.wait_recv()
    own_rows = pl.ds(pl.multiple_of(y * TOK, TOK), TOK)
    proj_v[own_rows, :] = (part_v[core] + other_v[...]).astype(BF16)
    gather = [
        remote(proj_v.at[own_rows], proj_v.at[own_rows], y_s.at[k - 1], y_r.at[k - 1], at_y(k)) for k in (2, 1, 3)
    ]
    for c in gather:
        c.start()
    for c in gather:
        c.wait_recv()

    def place(i, j, first_row, rows):
        base = ((z + STEPS[i] + NZ) % NZ) * UNIT + ((x + j + NX) % NX) * ROWS + first_row
        return pl.ds(pl.multiple_of(base, 32), rows)

    def x_rows(i, j):
        return place(i, j, 0, RX)

    def z_rows(i, j):
        return place(i, j, RX, RZ)

    def compute(i):
        cot_in[i].wait()
        cot_x[i].wait_recv()
        term[unit_cols(i), :] = dot(cot_v[:, unit_cols(i)], proj_v[...], ((0,), (0,))).astype(BF16)

    sends = list(cot_x) + [swap] + gather

    def start(copy):
        copy.start()
        sends.append(copy)
        return copy

    x_first = {}

    def x_open(i):
        s = 1 - 2 * (i % 2)
        x_first[i, 0] = start(
            remote(term.at[x_rows(i, 2 * s)], xr.at[i, 0], xr_s.at[i, 0], xr_r.at[i, 0], at_x(s))
        )
        x_first[i, 2] = start(
            remote(term.at[x_rows(i, -s)], xr.at[i, 2], xr_s.at[i, 2], xr_r.at[i, 2], at_x(-s))
        )

    def x_forward(i):
        s = 1 - 2 * (i % 2)
        x_first[i, 0].wait_recv()
        rows = x_rows(i, s)
        term[rows, :] = term[rows, :] + xr[i, 0]
        x_first[i, 1] = start(remote(term.at[rows], xr.at[i, 1], xr_s.at[i, 1], xr_r.at[i, 1], at_x(s)))

    zx_copies = {}

    def x_close(i):
        x_first[i, 1].wait_recv()
        x_first[i, 2].wait_recv()
        rows = x_rows(i, 0)
        total = term[rows, :].astype(F32) + xr[i, 1].astype(F32) + xr[i, 2].astype(F32)
        if i == 0:
            term[rows, :] = total.astype(BF16)
            for n, (s, lanes) in enumerate(((1, pl.ds(0, QUARTER)), (-1, pl.ds(QUARTER, QUARTER)))):
                zx_copies[0, s] = start(
                    remote(term.at[rows, lanes], zx.at[0, :, lanes], zx_s.at[7 * n], zx_r.at[7 * n], at_z(s))
                )
            return None
        if i == 7:
            zx_copies[5].wait_recv()
            zx_copies[6].wait_recv()
            return total + zx[5].astype(F32) + zx[6].astype(F32)
        s = 1 if STEPS[i] > 0 else -1
        if i in (1, 2):
            lanes = slice(0, QUARTER) if s == 1 else slice(QUARTER, HALF)
            rest = slice(QUARTER, HALF) if s == 1 else slice(0, QUARTER)
            zx_copies[0, s].wait_recv()
            term[rows, lanes] = (total[:, lanes] + zx[0, :, lanes].astype(F32)).astype(BF16)
            term[rows, rest] = total[:, rest].astype(BF16)
        else:
            zx_copies[i - 2].wait_recv()
            term[rows, :] = (total + zx[i - 2].astype(F32)).astype(BF16)
        zx_copies[i] = start(remote(term.at[rows], zx.at[i], zx_s.at[i], zx_r.at[i], at_z(s)))
        return None

    zz_copies = {}

    def z_step(i, j):
        s = 1 if STEPS[i] > 0 else -1
        rows = z_rows(i, j)
        if i == 0:
            s = 1 if j < 2 else -1
        elif i in (1, 2):
            if (j < 2) == (s == 1):
                zz_copies[0, j].wait_recv()
                term[rows, :] = term[rows, :] + zz[0, j]
        else:
            zz_copies[i - 2, j].wait_recv()
            term[rows, :] = term[rows, :] + zz[i - 2, j]
        zz_copies[i, j] = start(remote(term.at[rows], zz.at[i, j], zz_s.at[i, j], zz_r.at[i, j], at_z(s)))

    def z_total(j):
        zz_copies[5, j].wait_recv()
        zz_copies[6, j].wait_recv()
        return term[z_rows(7, j), :].astype(F32) + zz[5, j].astype(F32) + zz[6, j].astype(F32)

    xz_copies = {}

    def z_open():
        rows = z_rows(7, 2)
        term[rows, :] = z_total(2).astype(BF16)
        for n, (s, lanes) in enumerate(((1, pl.ds(0, QUARTER)), (-1, pl.ds(QUARTER, QUARTER)))):
            xz_copies[0, s] = start(
                remote(term.at[rows, lanes], xz.at[0, :, lanes], xz_s.at[3 * n], xz_r.at[3 * n], at_x(s))
            )

    def z_forward(n):
        s = 1 if n == 1 else -1
        j = s % NX
        total = z_total(j)
        lanes = slice(0, QUARTER) if s == 1 else slice(QUARTER, HALF)
        rest = slice(QUARTER, HALF) if s == 1 else slice(0, QUARTER)
        rows = z_rows(7, j)
        xz_copies[0, s].wait_recv()
        term[rows, lanes] = (total[:, lanes] + xz[0, :, lanes].astype(F32)).astype(BF16)
        term[rows, rest] = total[:, rest].astype(BF16)
        xz_copies[n] = start(remote(term.at[rows], xz.at[n], xz_s.at[n], xz_r.at[n], at_x(s)))

    def z_close():
        total = z_total(0)
        xz_copies[1].wait_recv()
        xz_copies[2].wait_recv()
        return total + xz[1].astype(F32) + xz[2].astype(F32)

    dir_copies = []
    own_lanes = pl.ds(pl.multiple_of(core * HALF, HALF), HALF)

    def adam(lowrank, rows):
        fresh_first = beta_first * first_v[rows, :] + (1.0 - beta_first) * lowrank
        fresh_second = beta_second * second_v[rows, :] + (1.0 - beta_second) * lowrank * lowrank
        new_first[rows, :] = fresh_first
        new_second[rows, :] = fresh_second
        direction = fresh_first / bias_first / (jnp.sqrt(fresh_second / bias_second) + adam_eps)
        dir_v[rows, own_lanes] = direction.astype(BF16)
        n = len(dir_copies)
        dir_copies.append(
            start(
                remote(dir_v.at[rows, own_lanes], dir_v.at[rows, own_lanes], dir_s.at[n], dir_r.at[n], sibling)
            )
        )

    run = {
        "C": compute, "X": x_open, "F": x_forward, "L": x_close, "Z": z_step, "O": z_open, "G": z_forward,
    }
    for name in ORDER:
        run[name[0]](*map(int, name[1:]))
    for c in loads[1 + KCH :]:
        c.wait()
    z_rows_own, x_rows_own = pl.ds(RX, RZ), pl.ds(0, RX)
    adam(z_close(), z_rows_own)
    adam(x_close(7), x_rows_own)
    for c in dir_copies:
        c.wait_recv()
    for c in sends:
        c.wait_send()


def back_project(
    direction, projector, fresh_first, fresh_second, upd, new_first, new_second,
    dir_v, prj_v, upd_v, kept_v, load, store, keep,
):
    kept = [
        pltpu.make_async_copy(fresh_first, kept_v.at[0], keep.at[0]),
        pltpu.make_async_copy(fresh_second, kept_v.at[1], keep.at[1]),
    ]
    loads = [pltpu.make_async_copy(direction, dir_v, load.at[0])]
    parts = [pl.ds(c * COLS, COLS) for c in range(WIDTH // COLS)]
    for c, part in enumerate(parts):
        loads.append(pltpu.make_async_copy(projector.at[part], prj_v.at[part], load.at[1 + c]))
    for c in loads + kept:
        c.start()
    loads[0].wait()
    stores = [
        pltpu.make_async_copy(kept_v.at[0], new_first.at[0, 0], keep.at[2]),
        pltpu.make_async_copy(kept_v.at[1], new_second.at[0, 0], keep.at[3]),
    ]
    for c, part in enumerate(parts):
        loads[1 + c].wait()
        upd_v[:, part] = dot(dir_v[...], prj_v[part, :], ((1,), (1,)))
        stores.append(pltpu.make_async_copy(upd_v.at[:, part], upd.at[0, 0, :, part], store.at[c]))
        stores[-1].start()
    for c in kept:
        c.wait()
    for c in stores[:2]:
        c.start()
    for c in stores:
        c.wait()


def per_device(activations, cotangents, projector, first_moment, second_moment):
    any_space = pl.BlockSpec(memory_space=pl.ANY)
    vmem = pl.BlockSpec(memory_space=pltpu.VMEM)
    dma = pltpu.SemaphoreType.DMA
    direction, fresh_first, fresh_second = pl.pallas_call(
        kernel,
        out_shape=(
            jax.ShapeDtypeStruct((ROWS, RANK), BF16),
            jax.ShapeDtypeStruct((ROWS, HALF), F32),
            jax.ShapeDtypeStruct((ROWS, HALF), F32),
        ),
        in_specs=[any_space] * 5,
        out_specs=(vmem, vmem, vmem),
        scratch_shapes=[
            pltpu.VMEM((TOK, WIDTH), BF16),
            pltpu.VMEM((WIDTH, RANK), BF16),
            pltpu.VMEM((512, HID), BF16),
            pltpu.VMEM((2, TOK, HALF), F32),
            pltpu.VMEM((TOK, HALF), F32),
            pltpu.VMEM((512, HALF), BF16),
            pltpu.VMEM((HID, HALF), BF16),
            pltpu.VMEM((8, 3, RX, HALF), BF16),
            pltpu.VMEM((7, NX, RZ, HALF), BF16),
            pltpu.VMEM((7, RX, HALF), BF16),
            pltpu.VMEM((3, RZ, HALF), BF16),
            pltpu.VMEM((ROWS, HALF), F32),
            pltpu.VMEM((ROWS, HALF), F32),
            dma((3 + KCH,)),
            dma((8,)),
            dma((8,)),
            dma((8,)),
            dma((1,)),
            dma((1,)),
            dma((3,)),
            dma((3,)),
            dma((8, 3)),
            dma((8, 3)),
            dma((7, NX)),
            dma((7, NX)),
            dma((8,)),
            dma((8,)),
            dma((4,)),
            dma((4,)),
            dma((2,)),
            dma((2,)),
        ],
        compiler_params=pltpu.CompilerParams(
            collective_id=0, has_side_effects=True, vmem_limit_bytes=56 * 2**20
        ),
        name="galore_step",
    )(activations, cotangents, projector, first_moment, second_moment)
    return pl.pallas_call(
        back_project,
        out_shape=(
            jax.ShapeDtypeStruct((1, 1, ROWS, WIDTH), F32),
            jax.ShapeDtypeStruct((1, 1, ROWS, HALF), F32),
            jax.ShapeDtypeStruct((1, 1, ROWS, HALF), F32),
        ),
        in_specs=[any_space] * 4,
        out_specs=(any_space,) * 3,
        scratch_shapes=[
            pltpu.VMEM((ROWS, RANK), BF16),
            pltpu.VMEM((WIDTH, RANK), BF16),
            pltpu.VMEM((ROWS, WIDTH), F32),
            pltpu.VMEM((2, ROWS, HALF), F32),
            dma((1 + WIDTH // COLS,)),
            dma((WIDTH // COLS,)),
            dma((4,)),
        ],
        compiler_params=pltpu.CompilerParams(vmem_limit_bytes=56 * 2**20),
        name="back_project",
    )(direction, projector, fresh_first, fresh_second)


def solution(mesh):
    return jax.shard_map(
        per_device,
        mesh=mesh,
        in_specs=(
            P(None, ("dp", "tensor"), "fsdp"),
            P(None, ("dp", "fsdp"), "tensor"),
            P("fsdp", None),
            P(None, "tensor", "dp", "fsdp"),
            P(None, "tensor", "dp", "fsdp"),
        ),
        out_specs=(
            P(None, "tensor", "dp", "fsdp"),
            P(None, "tensor", "dp", "fsdp"),
            P(None, "tensor", "dp", "fsdp"),
        ),
        check_vma=False,
    )
```

```python
import functools

import jax
import jax.numpy as jnp
from jax import lax
from jax.experimental import pallas as pl
from jax.experimental.pallas import tpu as pltpu
from jax.sharding import PartitionSpec as P

beta_first = 0.9
beta_second = 0.999
bias_first = 1.0 - 0.9**10
bias_second = 1.0 - 0.999**10
adam_eps = 1e-08

NZ, NX, NY = 8, 4, 4
TOK = 128
WIDTH = 4096
RANK = 1024
HALF = 512
ROWS = 224
UNIT = NX * ROWS
HID = NZ * UNIT
RX = 128
RZ = ROWS - RX
LANES = HALF // 2
COLS = 512
F32, BF16 = jnp.float32, jnp.bfloat16
MESH = pl.DeviceIdType.MESH

STEPS = (4, 3, -3, 2, -2, 1, -1, 0)

ORDER = (
    "C00", "X00", "Z004", "Z005", "C10", "Z105", "X10", "C20", "C01", "Z015", "Z204", "X01", "C11", "C31",
    "Z104", "Z205", "X11", "C30", "C40", "X20", "Z014", "C21", "X21", "X30", "Z115", "F02", "X31", "Z215",
    "Z214", "C41", "X42", "Z305", "F12", "C52", "C72", "Z404", "F20", "X72", "Z304", "C62", "Z114", "F21",
    "X62", "Z405", "X52", "Z315", "Z415", "F32", "L02", "Z414", "Z314", "F40", "F41", "Z525", "Z625", "F72",
    "L12", "Z524", "L22", "Z624", "F50", "F51", "F60", "F61", "O72", "L31", "L30", "L40", "L41", "L51",
    "G272", "L60", "G172", "L50", "L61", "L70", "H72", "L71",
)


def dot(a, b, dims):
    return lax.dot_general(a, b, (dims, ((), ())), preferred_element_type=F32)


def kernel(
    act, cot, projector, first, second, dir_v, new_first, new_second,
    act_v, prj_v, cot_v, part_v, other_v, proj_v, tx, tz, xr, zz, zx, xz, first_v, second_v,
    load, cot_load, cot_s, cot_r, part_s, part_r, y_s, y_r, xr_s, xr_r, zz_s, zz_r,
    zx_s, zx_r, xz_s, xz_r, dir_s, dir_r,
):
    dp, core, y = lax.axis_index("dp"), lax.axis_index("fsdp"), lax.axis_index("tensor")
    z, x = dp // NX, dp % NX

    def at_x(k):
        return (z * NX + (x + k + NX) % NX, core, y)

    def at_z(k):
        return (((z + k + NZ) % NZ) * NX + x, core, y)

    def at_y(k):
        return (dp, core, (y + k) % NY)

    sibling = (dp, 1 - core, y)

    def remote(src, dst, send, recv, device):
        return pltpu.make_async_remote_copy(
            src_ref=src, dst_ref=dst, send_sem=send, recv_sem=recv, device_id=device, device_id_type=MESH
        )

    def unit_cols(i):
        return pl.ds(pl.multiple_of(((z + STEPS[i] + NZ) % NZ) * UNIT, UNIT), UNIT)

    own_tok = pl.ds(pl.multiple_of(core * 256, 256), 256)
    get_act = pltpu.make_async_copy(act.at[0], act_v, load.at[0])
    get_act.start()
    get_prj = []
    for r in range(2):
        for h in range(2):
            cols = pl.ds(h * HALF + r * LANES, LANES)
            get_prj.append(pltpu.make_async_copy(projector.at[:, cols], prj_v.at[r, h], load.at[1 + 2 * r + h]))
            get_prj[-1].start()
    get_moments = [
        pltpu.make_async_copy(first.at[0, 0], first_v, load.at[5]),
        pltpu.make_async_copy(second.at[0, 0], second_v, load.at[6]),
    ]
    cot_in = [
        pltpu.make_async_copy(cot.at[0, :, unit_cols(i)], cot_v.at[own_tok, unit_cols(i)], cot_load.at[i])
        for i in range(NZ)
    ]
    cot_x = [
        remote(
            cot_v.at[own_tok, unit_cols(i)], cot_v.at[own_tok, unit_cols(i)], cot_s.at[i], cot_r.at[i], sibling
        )
        for i in range(NZ)
    ]

    barrier = pltpu.get_barrier_semaphore()
    for device in (sibling, at_y(1), at_y(2), at_y(3), at_x(1), at_x(-1), at_z(1), at_z(-1)):
        pl.semaphore_signal(barrier, inc=1, device_id=device, device_id_type=MESH)
    pl.semaphore_wait(barrier, 8)

    swap = [
        remote(part_v.at[r, 1 - core], other_v.at[r], part_s.at[r], part_r.at[r], sibling) for r in range(2)
    ]
    own_rows = pl.ds(pl.multiple_of(y * TOK, TOK), TOK)
    gather = [
        [
            remote(proj_v.at[r, own_rows], proj_v.at[r, own_rows], y_s.at[r, k - 1], y_r.at[r, k - 1], at_y(k))
            for k in (2, 1, 3)
        ]
        for r in range(2)
    ]
    get_act.wait()
    for r in range(2):
        for h in range(2):
            get_prj[2 * r + h].wait()
        if r == 1:
            for c in cot_in + get_moments:
                c.start()
        part_v[r, 1 - core] = dot(act_v[...], prj_v[r, 1 - core], ((1,), (0,)))
        swap[r].start()
        part_v[r, core] = dot(act_v[...], prj_v[r, core], ((1,), (0,)))
        swap[r].wait_recv()
        proj_v[r, own_rows, :] = (part_v[r, core] + other_v[r]).astype(BF16)
        for c in gather[r]:
            c.start()
    for i in range(NZ):
        cot_in[i].wait()
        cot_x[i].start()

    sends = cot_x + swap + gather[0] + gather[1]
    pending = {}

    def send(key, src, dst, send_sem, recv_sem, device):
        copy = remote(src, dst, send_sem, recv_sem, device)
        copy.start()
        sends.append(copy)
        pending[key] = copy

    def parts(r):
        return (0, 1) if r == 2 else (r,)

    def pick(r):
        return slice(None) if r == 2 else r

    def need(kind, r):
        for half in parts(r) + (2,):
            copy = pending.pop(kind + (half,), None)
            if copy is not None:
                copy.wait_recv()

    gathered, exchanged = set(), set()

    def compute(i, r):
        if i not in exchanged:
            exchanged.add(i)
            cot_x[i].wait_recv()
        for half in parts(r):
            if half not in gathered:
                gathered.add(half)
                for c in gather[half]:
                    c.wait_recv()
            block = dot(cot_v[:, unit_cols(i)], proj_v[half], ((0,), (0,))).astype(BF16)
            for column in range(NX):
                j, first_row = (column - x + NX) % NX, column * ROWS
                tx[half, i, j] = block[first_row : first_row + RX]
                tz[half, i, j] = block[first_row + RX : first_row + ROWS]

    def x_send(i, r, n, j, k):
        h = r % 2
        send(
            ("x", i, n, r), tx.at[pick(r), i, j % NX], xr.at[pick(r), i, n],
            xr_s.at[h, i, n], xr_r.at[h, i, n], at_x(k),
        )

    def x_open(i, r):
        s = 1 - 2 * (i % 2)
        x_send(i, r, 0, 2, s)
        x_send(i, r, 2, -s, -s)

    def x_forward(i, r):
        s = 1 - 2 * (i % 2)
        need(("x", i, 0), r)
        for half in parts(r):
            tx[half, i, s % NX] = tx[half, i, s % NX] + xr[half, i, 0]
        x_send(i, r, 1, s, s)

    def x_close(i, r):
        s = 1 if STEPS[i] > 0 else -1
        need(("x", i, 1), r)
        need(("x", i, 2), r)
        earlier = {0: (), 1: (0,), 2: (0,), 7: (5, 6)}.get(i, (i - 2,))
        for e in earlier:
            need(("zx", e), r if e else (0 if s == 1 else 1))
        for half in parts(r):
            total = tx[half, i, 0].astype(F32) + xr[half, i, 1].astype(F32) + xr[half, i, 2].astype(F32)
            for e in earlier:
                if e or (half == 0) == (s == 1):
                    total = total + zx[half, e].astype(F32)
            if i == 7:
                adam(total, pl.ds(0, RX), half, 0)
            else:
                tx[half, i, 0] = total.astype(BF16)
        if i == 0:
            for h, k in enumerate((1, -1)):
                send(("zx", 0, h), tx.at[h, 0, 0], zx.at[h, 0], zx_s.at[h, 0], zx_r.at[h, 0], at_z(k))
        elif i < 7:
            h = r % 2
            send(("zx", i, r), tx.at[pick(r), i, 0], zx.at[pick(r), i], zx_s.at[h, i], zx_r.at[h, i], at_z(s))

    def z_step(i, r, g):
        first, count = ((g - 4) * 2, 2) if g > 3 else (g, 1)
        s = 1 if STEPS[i] > 0 else -1
        if i == 0:
            s = 1 if first < 2 else -1
        elif i > 2 or (first < 2) == (s == 1):
            e = max(i - 2, 0)
            for j in range(first, first + count):
                need_z(e, j, r)
                for half in parts(r):
                    tz[half, i, j] = tz[half, i, j] + zz[half, e, j]
        h, blocks = r % 2, pl.ds(first, count)
        send(
            ("z", i, g, r), tz.at[pick(r), i, blocks], zz.at[pick(r), i, blocks],
            zz_s.at[h, i, first], zz_r.at[h, i, first], at_z(s),
        )

    def need_z(e, j, r):
        need(("z", e, j), r)
        need(("z", e, 4 + j // 2), r)

    def z_total(j, half):
        for e in (5, 6):
            need_z(e, j, 2)
        return tz[half, 7, j].astype(F32) + zz[half, 5, j].astype(F32) + zz[half, 6, j].astype(F32)

    def z_open(i, r):
        for h, k in enumerate((1, -1)):
            tz[h, 7, 2] = z_total(2, h).astype(BF16)
            send(("xz", 0, h), tz.at[h, 7, 2], xz.at[h, 0], xz_s.at[h, 0], xz_r.at[h, 0], at_x(k))

    def z_forward(n, i, r):
        s = 1 if n == 1 else -1
        j = s % NX
        need(("xz", 0), 0 if s == 1 else 1)
        for half in range(2):
            total = z_total(j, half)
            if (half == 0) == (s == 1):
                total = total + xz[half, 0].astype(F32)
            tz[half, 7, j] = total.astype(BF16)
        send(("xz", n, 2), tz.at[:, 7, j], xz.at[:, n], xz_s.at[0, n], xz_r.at[0, n], at_x(s))

    def z_close(i, r):
        for n in (1, 2):
            need(("xz", n), 2)
        for half in range(2):
            total = z_total(0, half)
            adam(total + xz[half, 1].astype(F32) + xz[half, 2].astype(F32), pl.ds(RX, RZ), half, 1)


    def adam(lowrank, rows, r, n):
        lanes = pl.ds(r * LANES, LANES)
        for c in get_moments:
            c.wait()
        get_moments.clear()
        fresh_first = beta_first * first_v[rows, lanes] + (1.0 - beta_first) * lowrank
        fresh_second = beta_second * second_v[rows, lanes] + (1.0 - beta_second) * lowrank * lowrank
        new_first[rows, lanes] = fresh_first
        new_second[rows, lanes] = fresh_second
        direction = fresh_first / bias_first / (jnp.sqrt(fresh_second / bias_second) + adam_eps)
        own = pl.ds(pl.multiple_of(core * HALF + r * LANES, LANES), LANES)
        dir_v[rows, own] = direction.astype(BF16)
        send(
            ("dir", n, r), dir_v.at[rows, own], dir_v.at[rows, own], dir_s.at[r, n], dir_r.at[r, n], sibling
        )

    run = {
        "C": compute, "X": x_open, "F": x_forward, "L": x_close,
        "Z": z_step, "O": z_open, "G": z_forward, "H": z_close,
    }
    for name in ORDER:
        run[name[0]](*map(int, name[1:]))
    for n in range(2):
        need(("dir", n), 2)
    assert not pending
    for c in sends:
        c.wait_send()


def back_project(
    direction, projector, fresh_first, fresh_second, upd, new_first, new_second,
    dir_v, prj_v, upd_v, kept_v, load, store, keep,
):
    kept = [
        pltpu.make_async_copy(fresh_first, kept_v.at[0], keep.at[0]),
        pltpu.make_async_copy(fresh_second, kept_v.at[1], keep.at[1]),
    ]
    loads = [pltpu.make_async_copy(direction, dir_v, load.at[0])]
    parts = [pl.ds(c * COLS, COLS) for c in range(WIDTH // COLS)]
    for c, part in enumerate(parts):
        loads.append(pltpu.make_async_copy(projector.at[part], prj_v.at[part], load.at[1 + c]))
    for c in loads + kept:
        c.start()
    loads[0].wait()
    stores = [
        pltpu.make_async_copy(kept_v.at[0], new_first.at[0, 0], keep.at[2]),
        pltpu.make_async_copy(kept_v.at[1], new_second.at[0, 0], keep.at[3]),
    ]
    for c, part in enumerate(parts):
        loads[1 + c].wait()
        upd_v[:, part] = dot(dir_v[...], prj_v[part, :], ((1,), (1,)))
        stores.append(pltpu.make_async_copy(upd_v.at[:, part], upd.at[0, 0, :, part], store.at[c]))
        stores[-1].start()
    for c in kept:
        c.wait()
    for c in stores[:2]:
        c.start()
    for c in stores:
        c.wait()


def per_device(activations, cotangents, projector, first_moment, second_moment):
    any_space = pl.BlockSpec(memory_space=pl.ANY)
    vmem = pl.BlockSpec(memory_space=pltpu.VMEM)
    dma = pltpu.SemaphoreType.DMA
    direction, fresh_first, fresh_second = pl.pallas_call(
        kernel,
        out_shape=(
            jax.ShapeDtypeStruct((ROWS, RANK), BF16),
            jax.ShapeDtypeStruct((ROWS, HALF), F32),
            jax.ShapeDtypeStruct((ROWS, HALF), F32),
        ),
        in_specs=[any_space] * 5,
        out_specs=(vmem, vmem, vmem),
        scratch_shapes=[
            pltpu.VMEM((TOK, WIDTH), BF16),
            pltpu.VMEM((2, 2, WIDTH, LANES), BF16),
            pltpu.VMEM((512, HID), BF16),
            pltpu.VMEM((2, 2, TOK, LANES), F32),
            pltpu.VMEM((2, TOK, LANES), F32),
            pltpu.VMEM((2, 512, LANES), BF16),
            pltpu.VMEM((2, 8, NX, RX, LANES), BF16),
            pltpu.VMEM((2, 8, NX, RZ, LANES), BF16),
            pltpu.VMEM((2, 8, 3, RX, LANES), BF16),
            pltpu.VMEM((2, 7, NX, RZ, LANES), BF16),
            pltpu.VMEM((2, 7, RX, LANES), BF16),
            pltpu.VMEM((2, 3, RZ, LANES), BF16),
            pltpu.VMEM((ROWS, HALF), F32),
            pltpu.VMEM((ROWS, HALF), F32),
            dma((7,)),
            dma((8,)),
            dma((8,)),
            dma((8,)),
            dma((2,)),
            dma((2,)),
            dma((2, 3)),
            dma((2, 3)),
            dma((2, 8, 3)),
            dma((2, 8, 3)),
            dma((2, 7, NX)),
            dma((2, 7, NX)),
            dma((2, 8)),
            dma((2, 8)),
            dma((2, 4)),
            dma((2, 4)),
            dma((2, 2)),
            dma((2, 2)),
        ],
        compiler_params=pltpu.CompilerParams(
            collective_id=0, has_side_effects=True, vmem_limit_bytes=56 * 2**20
        ),
        name="galore_step",
    )(activations, cotangents, projector, first_moment, second_moment)
    return pl.pallas_call(
        back_project,
        out_shape=(
            jax.ShapeDtypeStruct((1, 1, ROWS, WIDTH), F32),
            jax.ShapeDtypeStruct((1, 1, ROWS, HALF), F32),
            jax.ShapeDtypeStruct((1, 1, ROWS, HALF), F32),
        ),
        in_specs=[any_space] * 4,
        out_specs=(any_space,) * 3,
        scratch_shapes=[
            pltpu.VMEM((ROWS, RANK), BF16),
            pltpu.VMEM((WIDTH, RANK), BF16),
            pltpu.VMEM((ROWS, WIDTH), F32),
            pltpu.VMEM((2, ROWS, HALF), F32),
            dma((1 + WIDTH // COLS,)),
            dma((WIDTH // COLS,)),
            dma((4,)),
        ],
        compiler_params=pltpu.CompilerParams(vmem_limit_bytes=56 * 2**20),
        name="back_project",
    )(direction, projector, fresh_first, fresh_second)


def solution(mesh):
    return jax.shard_map(
        per_device,
        mesh=mesh,
        in_specs=(
            P(None, ("dp", "tensor"), "fsdp"),
            P(None, ("dp", "fsdp"), "tensor"),
            P("fsdp", None),
            P(None, "tensor", "dp", "fsdp"),
            P(None, "tensor", "dp", "fsdp"),
        ),
        out_specs=(
            P(None, "tensor", "dp", "fsdp"),
            P(None, "tensor", "dp", "fsdp"),
            P(None, "tensor", "dp", "fsdp"),
        ),
        check_vma=False,
    )
```

```python
import functools

import jax
import jax.numpy as jnp
from jax import lax
from jax.experimental import pallas as pl
from jax.experimental.pallas import tpu as pltpu
from jax.sharding import PartitionSpec as P

beta_first = 0.9
beta_second = 0.999
bias_first = 1.0 - 0.9**10
bias_second = 1.0 - 0.999**10
adam_eps = 1e-08

NZ, NX, NY = 8, 4, 4
TOK = 128
WIDTH = 4096
RANK = 1024
HALF = 512
ROWS = 224
UNIT = NX * ROWS
HID = NZ * UNIT
RX = 128
RZ = ROWS - RX
LANES = HALF // 2
COLS = 512
F32, BF16 = jnp.float32, jnp.bfloat16
MESH = pl.DeviceIdType.MESH

STEPS = (4, 3, -3, 2, -2, 1, -1, 0)

ORDER = (
    "C00", "X00", "Z004", "Z005", "C10", "Z105", "X10", "C20", "C01", "Z015", "Z204", "X01", "C11", "C31",
    "Z104", "Z205", "X11", "C30", "C40", "X20", "Z014", "C21", "X21", "X30", "Z115", "F02", "X31", "Z215",
    "Z214", "C41", "X42", "Z305", "F12", "C52", "C72", "Z404", "F20", "X72", "Z304", "C62", "Z114", "F21",
    "X62", "Z405", "X52", "Z315", "Z415", "F32", "L02", "Z414", "Z314", "F40", "F41", "Z525", "Z625", "F72",
    "L12", "Z524", "L22", "Z624", "F50", "F51", "F60", "F61", "O72", "L31", "L30", "L40", "L41", "L51",
    "G272", "L60", "G172", "L50", "L61", "L70", "H72", "L71",
)


def dot(a, b, dims):
    return lax.dot_general(a, b, (dims, ((), ())), preferred_element_type=F32)


def kernel(
    act, cot, projector, first, second, dir_v, new_first, new_second,
    act_v, prj_v, cot_v, part_v, other_v, proj_v, tx, tz, xr, zz, zx, xz, first_v, second_v,
    load, cot_load, cot_s, cot_r, part_s, part_r, y_s, y_r, xr_s, xr_r, zz_s, zz_r,
    zx_s, zx_r, xz_s, xz_r, dir_s, dir_r,
):
    dp, core, y = lax.axis_index("dp"), lax.axis_index("fsdp"), lax.axis_index("tensor")
    z, x = dp // NX, dp % NX

    def at_x(k):
        return (z * NX + (x + k + NX) % NX, core, y)

    def at_z(k):
        return (((z + k + NZ) % NZ) * NX + x, core, y)

    def at_y(k):
        return (dp, core, (y + k) % NY)

    sibling = (dp, 1 - core, y)

    def remote(src, dst, send, recv, device):
        return pltpu.make_async_remote_copy(
            src_ref=src, dst_ref=dst, send_sem=send, recv_sem=recv, device_id=device, device_id_type=MESH
        )

    def unit_cols(i):
        return pl.ds(pl.multiple_of(((z + STEPS[i] + NZ) % NZ) * UNIT, UNIT), UNIT)

    own_tok = pl.ds(pl.multiple_of(core * 256, 256), 256)
    get_act = pltpu.make_async_copy(act.at[0], act_v, load.at[0])
    get_act.start()
    get_prj = []
    for r in range(2):
        for h in range(2):
            cols = pl.ds(h * HALF + r * LANES, LANES)
            get_prj.append(pltpu.make_async_copy(projector.at[:, cols], prj_v.at[r, h], load.at[1 + 2 * r + h]))
            if r == 0:
                get_prj[-1].start()
    get_moments = [
        pltpu.make_async_copy(first.at[0, 0], first_v, load.at[5]),
        pltpu.make_async_copy(second.at[0, 0], second_v, load.at[6]),
    ]
    cot_in = [
        pltpu.make_async_copy(cot.at[0, :, unit_cols(i)], cot_v.at[own_tok, unit_cols(i)], cot_load.at[i])
        for i in range(NZ)
    ]
    cot_x = [
        remote(
            cot_v.at[own_tok, unit_cols(i)], cot_v.at[own_tok, unit_cols(i)], cot_s.at[i], cot_r.at[i], sibling
        )
        for i in range(NZ)
    ]

    barrier = pltpu.get_barrier_semaphore()
    for device in (sibling, at_y(1), at_y(2), at_y(3), at_x(1), at_x(-1), at_z(1), at_z(-1)):
        pl.semaphore_signal(barrier, inc=1, device_id=device, device_id_type=MESH)
    pl.semaphore_wait(barrier, 8)

    swap = [
        remote(part_v.at[r, 1 - core], other_v.at[r], part_s.at[r], part_r.at[r], sibling) for r in range(2)
    ]
    own_rows = pl.ds(pl.multiple_of(y * TOK, TOK), TOK)
    gather = [
        [
            remote(proj_v.at[r, own_rows], proj_v.at[r, own_rows], y_s.at[r, k - 1], y_r.at[r, k - 1], at_y(k))
            for k in (2, 1, 3)
        ]
        for r in range(2)
    ]
    get_act.wait()
    for r in range(2):
        for h in range(2):
            get_prj[2 * r + h].wait()
        for c in (get_prj[2:] if r == 0 else cot_in + get_moments):
            c.start()
        part_v[r, 1 - core] = dot(act_v[...], prj_v[r, 1 - core], ((1,), (0,)))
        swap[r].start()
        part_v[r, core] = dot(act_v[...], prj_v[r, core], ((1,), (0,)))
        swap[r].wait_recv()
        proj_v[r, own_rows, :] = (part_v[r, core] + other_v[r]).astype(BF16)
        for c in gather[r]:
            c.start()
    for i in range(NZ):
        cot_in[i].wait()
        cot_x[i].start()

    sends = cot_x + swap + gather[0] + gather[1]
    pending = {}

    def send(key, src, dst, send_sem, recv_sem, device):
        copy = remote(src, dst, send_sem, recv_sem, device)
        copy.start()
        sends.append(copy)
        pending[key] = copy

    def parts(r):
        return (0, 1) if r == 2 else (r,)

    def pick(r):
        return slice(None) if r == 2 else r

    def need(kind, r):
        for half in parts(r) + (2,):
            copy = pending.pop(kind + (half,), None)
            if copy is not None:
                copy.wait_recv()

    gathered, exchanged = set(), set()

    def compute(i, r):
        if i not in exchanged:
            exchanged.add(i)
            cot_x[i].wait_recv()
        for half in parts(r):
            if half not in gathered:
                gathered.add(half)
                for c in gather[half]:
                    c.wait_recv()
            block = dot(cot_v[:, unit_cols(i)], proj_v[half], ((0,), (0,))).astype(BF16)
            for column in range(NX):
                j, first_row = (column - x + NX) % NX, column * ROWS
                tx[half, i, j] = block[first_row : first_row + RX]
                tz[half, i, j] = block[first_row + RX : first_row + ROWS]

    def x_send(i, r, n, j, k):
        h = r % 2
        send(
            ("x", i, n, r), tx.at[pick(r), i, j % NX], xr.at[pick(r), i, n],
            xr_s.at[h, i, n], xr_r.at[h, i, n], at_x(k),
        )

    def x_open(i, r):
        s = 1 - 2 * (i % 2)
        x_send(i, r, 0, 2, s)
        x_send(i, r, 2, -s, -s)

    def x_forward(i, r):
        s = 1 - 2 * (i % 2)
        need(("x", i, 0), r)
        for half in parts(r):
            tx[half, i, s % NX] = tx[half, i, s % NX] + xr[half, i, 0]
        x_send(i, r, 1, s, s)

    def x_close(i, r):
        s = 1 if STEPS[i] > 0 else -1
        need(("x", i, 1), r)
        need(("x", i, 2), r)
        earlier = {0: (), 1: (0,), 2: (0,), 7: (5, 6)}.get(i, (i - 2,))
        for e in earlier:
            need(("zx", e), r if e else (0 if s == 1 else 1))
        for half in parts(r):
            total = tx[half, i, 0].astype(F32) + xr[half, i, 1].astype(F32) + xr[half, i, 2].astype(F32)
            for e in earlier:
                if e or (half == 0) == (s == 1):
                    total = total + zx[half, e].astype(F32)
            if i == 7:
                adam(total, pl.ds(0, RX), half, 0)
            else:
                tx[half, i, 0] = total.astype(BF16)
        if i == 0:
            for h, k in enumerate((1, -1)):
                send(("zx", 0, h), tx.at[h, 0, 0], zx.at[h, 0], zx_s.at[h, 0], zx_r.at[h, 0], at_z(k))
        elif i < 7:
            h = r % 2
            send(("zx", i, r), tx.at[pick(r), i, 0], zx.at[pick(r), i], zx_s.at[h, i], zx_r.at[h, i], at_z(s))

    def z_step(i, r, g):
        first, count = ((g - 4) * 2, 2) if g > 3 else (g, 1)
        s = 1 if STEPS[i] > 0 else -1
        if i == 0:
            s = 1 if first < 2 else -1
        elif i > 2 or (first < 2) == (s == 1):
            e = max(i - 2, 0)
            for j in range(first, first + count):
                need_z(e, j, r)
                for half in parts(r):
                    tz[half, i, j] = tz[half, i, j] + zz[half, e, j]
        h, blocks = r % 2, pl.ds(first, count)
        send(
            ("z", i, g, r), tz.at[pick(r), i, blocks], zz.at[pick(r), i, blocks],
            zz_s.at[h, i, first], zz_r.at[h, i, first], at_z(s),
        )

    def need_z(e, j, r):
        need(("z", e, j), r)
        need(("z", e, 4 + j // 2), r)

    def z_total(j, half):
        for e in (5, 6):
            need_z(e, j, 2)
        return tz[half, 7, j].astype(F32) + zz[half, 5, j].astype(F32) + zz[half, 6, j].astype(F32)

    def z_open(i, r):
        for h, k in enumerate((1, -1)):
            tz[h, 7, 2] = z_total(2, h).astype(BF16)
            send(("xz", 0, h), tz.at[h, 7, 2], xz.at[h, 0], xz_s.at[h, 0], xz_r.at[h, 0], at_x(k))

    def z_forward(n, i, r):
        s = 1 if n == 1 else -1
        j = s % NX
        need(("xz", 0), 0 if s == 1 else 1)
        for half in range(2):
            total = z_total(j, half)
            if (half == 0) == (s == 1):
                total = total + xz[half, 0].astype(F32)
            tz[half, 7, j] = total.astype(BF16)
        send(("xz", n, 2), tz.at[:, 7, j], xz.at[:, n], xz_s.at[0, n], xz_r.at[0, n], at_x(s))

    def z_close(i, r):
        for n in (1, 2):
            need(("xz", n), 2)
        for half in range(2):
            total = z_total(0, half)
            adam(total + xz[half, 1].astype(F32) + xz[half, 2].astype(F32), pl.ds(RX, RZ), half, 1)


    def adam(lowrank, rows, r, n):
        lanes = pl.ds(r * LANES, LANES)
        for c in get_moments:
            c.wait()
        get_moments.clear()
        fresh_first = beta_first * first_v[rows, lanes] + (1.0 - beta_first) * lowrank
        fresh_second = beta_second * second_v[rows, lanes] + (1.0 - beta_second) * lowrank * lowrank
        new_first[rows, lanes] = fresh_first
        new_second[rows, lanes] = fresh_second
        direction = fresh_first / bias_first / (jnp.sqrt(fresh_second / bias_second) + adam_eps)
        own = pl.ds(pl.multiple_of(core * HALF + r * LANES, LANES), LANES)
        dir_v[rows, own] = direction.astype(BF16)
        send(
            ("dir", n, r), dir_v.at[rows, own], dir_v.at[rows, own], dir_s.at[r, n], dir_r.at[r, n], sibling
        )

    run = {
        "C": compute, "X": x_open, "F": x_forward, "L": x_close,
        "Z": z_step, "O": z_open, "G": z_forward, "H": z_close,
    }
    for name in ORDER:
        run[name[0]](*map(int, name[1:]))
    for n in range(2):
        need(("dir", n), 2)
    assert not pending
    for c in sends:
        c.wait_send()


def back_project(direction, projector, fresh_first, fresh_second, upd, new_first, new_second, upd_v, store):
    stores = [
        pltpu.make_async_copy(fresh_first, new_first.at[0, 0], store.at[0]),
        pltpu.make_async_copy(fresh_second, new_second.at[0, 0], store.at[1]),
    ]
    for c in stores:
        c.start()
    for c in range(WIDTH // COLS):
        part = pl.ds(c * COLS, COLS)
        upd_v[:, part] = dot(direction[...], projector[part, :], ((1,), (1,)))
        stores.append(pltpu.make_async_copy(upd_v.at[:, part], upd.at[0, 0, :, part], store.at[2 + c]))
        stores[-1].start()
    for c in stores:
        c.wait()


def per_device(activations, cotangents, projector, first_moment, second_moment):
    any_space = pl.BlockSpec(memory_space=pl.ANY)
    vmem = pl.BlockSpec(memory_space=pltpu.VMEM)
    dma = pltpu.SemaphoreType.DMA
    direction, fresh_first, fresh_second = pl.pallas_call(
        kernel,
        out_shape=(
            jax.ShapeDtypeStruct((ROWS, RANK), BF16),
            jax.ShapeDtypeStruct((ROWS, HALF), F32),
            jax.ShapeDtypeStruct((ROWS, HALF), F32),
        ),
        in_specs=[any_space] * 5,
        out_specs=(vmem, vmem, vmem),
        scratch_shapes=[
            pltpu.VMEM((TOK, WIDTH), BF16),
            pltpu.VMEM((2, 2, WIDTH, LANES), BF16),
            pltpu.VMEM((512, HID), BF16),
            pltpu.VMEM((2, 2, TOK, LANES), F32),
            pltpu.VMEM((2, TOK, LANES), F32),
            pltpu.VMEM((2, 512, LANES), BF16),
            pltpu.VMEM((2, 8, NX, RX, LANES), BF16),
            pltpu.VMEM((2, 8, NX, RZ, LANES), BF16),
            pltpu.VMEM((2, 8, 3, RX, LANES), BF16),
            pltpu.VMEM((2, 7, NX, RZ, LANES), BF16),
            pltpu.VMEM((2, 7, RX, LANES), BF16),
            pltpu.VMEM((2, 3, RZ, LANES), BF16),
            pltpu.VMEM((ROWS, HALF), F32),
            pltpu.VMEM((ROWS, HALF), F32),
            dma((7,)),
            dma((8,)),
            dma((8,)),
            dma((8,)),
            dma((2,)),
            dma((2,)),
            dma((2, 3)),
            dma((2, 3)),
            dma((2, 8, 3)),
            dma((2, 8, 3)),
            dma((2, 7, NX)),
            dma((2, 7, NX)),
            dma((2, 8)),
            dma((2, 8)),
            dma((2, 4)),
            dma((2, 4)),
            dma((2, 2)),
            dma((2, 2)),
        ],
        compiler_params=pltpu.CompilerParams(
            collective_id=0, has_side_effects=True, vmem_limit_bytes=105 * 2**19
        ),
        name="galore_step",
    )(activations, cotangents, projector, first_moment, second_moment)
    return pl.pallas_call(
        back_project,
        out_shape=(
            jax.ShapeDtypeStruct((1, 1, ROWS, WIDTH), F32),
            jax.ShapeDtypeStruct((1, 1, ROWS, HALF), F32),
            jax.ShapeDtypeStruct((1, 1, ROWS, HALF), F32),
        ),
        in_specs=[vmem] * 4,
        out_specs=(any_space,) * 3,
        scratch_shapes=[pltpu.VMEM((ROWS, WIDTH), F32), dma((2 + WIDTH // COLS,))],
        compiler_params=pltpu.CompilerParams(vmem_limit_bytes=12 * 2**20),
        name="back_project",
    )(direction, projector, fresh_first, fresh_second)


def solution(mesh):
    return jax.shard_map(
        per_device,
        mesh=mesh,
        in_specs=(
            P(None, ("dp", "tensor"), "fsdp"),
            P(None, ("dp", "fsdp"), "tensor"),
            P("fsdp", None),
            P(None, "tensor", "dp", "fsdp"),
            P(None, "tensor", "dp", "fsdp"),
        ),
        out_specs=(
            P(None, "tensor", "dp", "fsdp"),
            P(None, "tensor", "dp", "fsdp"),
            P(None, "tensor", "dp", "fsdp"),
        ),
        check_vma=False,
    )
```

```python
import functools

import jax
import jax.numpy as jnp
from jax import lax
from jax.experimental import pallas as pl
from jax.experimental.pallas import tpu as pltpu
from jax.sharding import PartitionSpec as P

beta_first = 0.9
beta_second = 0.999
bias_first = 1.0 - 0.9**10
bias_second = 1.0 - 0.999**10
adam_eps = 1e-08

NZ, NX, NY = 8, 4, 4
TOK = 128
WIDTH = 4096
RANK = 1024
HALF = 512
ROWS = 224
UNIT = NX * ROWS
HID = NZ * UNIT
RX = 128
RZ = ROWS - RX
LANES = HALF // 2
COLS = 512
F32, BF16 = jnp.float32, jnp.bfloat16
MESH = pl.DeviceIdType.MESH

STEPS = (4, 3, -3, 2, -2, 1, -1, 0)

ORDER = (
    "C00", "Z004", "X00", "Z005", "C10", "X10", "Z105", "C20", "C01", "Z015", "X01", "X20", "Z204", "C30",
    "Z014", "C11", "Z115", "X11", "C41", "C40", "Z205", "C21", "X21", "Z104", "F02", "X30", "C31", "Z215",
    "X31", "C62", "Z114", "Z305", "X42", "C72", "Z404", "F12", "X62", "C52", "Z315", "F22", "Z214", "Z405",
    "X72", "X52", "Z304", "Z415", "L02", "F32", "Z314", "Z414", "Z523", "Z522", "F40", "F41", "Z623", "Z622",
    "F60", "F61", "L12", "Z521", "Z520", "L22", "F70", "Z621", "Z620", "F71", "F50", "F51", "O72", "L30",
    "L31", "L40", "L41", "L50", "G172", "G272", "L60", "L51", "L61", "L70", "H72", "L71",
)


def dot(a, b, dims):
    return lax.dot_general(a, b, (dims, ((), ())), preferred_element_type=F32)


def kernel(
    act, cot, projector, first, second, dir_v, new_first, new_second,
    act_v, prj_v, cot_v, part_v, other_v, proj_v, tx, tz, xr, zz, zx, xz, first_v, second_v,
    load, cot_load, cot_s, cot_r, part_s, part_r, y_s, y_r, xr_s, xr_r, zz_s, zz_r,
    zx_s, zx_r, xz_s, xz_r, dir_s, dir_r,
):
    dp, core, y = lax.axis_index("dp"), lax.axis_index("fsdp"), lax.axis_index("tensor")
    z, x = dp // NX, dp % NX

    def at_x(k):
        return (z * NX + (x + k + NX) % NX, core, y)

    def at_z(k):
        return (((z + k + NZ) % NZ) * NX + x, core, y)

    def at_y(k):
        return (dp, core, (y + k) % NY)

    sibling = (dp, 1 - core, y)

    def remote(src, dst, send, recv, device):
        return pltpu.make_async_remote_copy(
            src_ref=src, dst_ref=dst, send_sem=send, recv_sem=recv, device_id=device, device_id_type=MESH
        )

    barrier = pltpu.get_barrier_semaphore()
    for device in (sibling, at_y(1), at_y(2), at_y(3), at_x(1), at_x(-1), at_z(1), at_z(-1)):
        pl.semaphore_signal(barrier, inc=1, device_id=device, device_id_type=MESH)

    def unit_cols(i):
        return pl.ds(pl.multiple_of(((z + STEPS[i] + NZ) % NZ) * UNIT, UNIT), UNIT)

    own_tok = pl.ds(pl.multiple_of(core * 256, 256), 256)
    get_act = pltpu.make_async_copy(act.at[0], act_v, load.at[0])
    get_act.start()
    get_prj = []
    for r in range(2):
        for h in range(2):
            cols = pl.ds(h * HALF + r * LANES, LANES)
            get_prj.append(pltpu.make_async_copy(projector.at[:, cols], prj_v.at[r, h], load.at[1 + 2 * r + h]))
            if r == 0:
                get_prj[-1].start()
    get_moments = [
        pltpu.make_async_copy(first.at[0, 0], first_v, load.at[5]),
        pltpu.make_async_copy(second.at[0, 0], second_v, load.at[6]),
    ]
    cot_in = [
        pltpu.make_async_copy(cot.at[0, :, unit_cols(i)], cot_v.at[own_tok, unit_cols(i)], cot_load.at[i])
        for i in range(NZ)
    ]
    cot_x = [
        remote(
            cot_v.at[own_tok, unit_cols(i)], cot_v.at[own_tok, unit_cols(i)], cot_s.at[i], cot_r.at[i], sibling
        )
        for i in range(NZ)
    ]

    pl.semaphore_wait(barrier, 8)

    swap = [
        remote(part_v.at[r, 1 - core], other_v.at[r], part_s.at[r], part_r.at[r], sibling) for r in range(2)
    ]
    own_rows = pl.ds(pl.multiple_of(y * TOK, TOK), TOK)
    gather = [
        [
            remote(proj_v.at[r, own_rows], proj_v.at[r, own_rows], y_s.at[r, k - 1], y_r.at[r, k - 1], at_y(k))
            for k in (2, 1, 3)
        ]
        for r in range(2)
    ]
    get_act.wait()
    for r in range(2):
        for h in range(2):
            get_prj[2 * r + h].wait()
        for c in (get_prj[2:] if r == 0 else cot_in + get_moments):
            c.start()
        part_v[r, 1 - core] = dot(act_v[...], prj_v[r, 1 - core], ((1,), (0,)))
        swap[r].start()
        part_v[r, core] = dot(act_v[...], prj_v[r, core], ((1,), (0,)))
        swap[r].wait_recv()
        proj_v[r, own_rows, :] = (part_v[r, core] + other_v[r]).astype(BF16)
        for c in gather[r]:
            c.start()
    for i in range(NZ):
        cot_in[i].wait()
        cot_x[i].start()

    sends = cot_x + swap + gather[0] + gather[1]
    pending = {}

    def send(key, src, dst, send_sem, recv_sem, device):
        copy = remote(src, dst, send_sem, recv_sem, device)
        copy.start()
        sends.append(copy)
        pending[key] = copy

    def parts(r):
        return (0, 1) if r == 2 else (r,)

    def pick(r):
        return slice(None) if r == 2 else r

    def need(kind, r):
        for half in parts(r) + (2,):
            copy = pending.pop(kind + (half,), None)
            if copy is not None:
                copy.wait_recv()

    gathered, exchanged = set(), set()

    def compute(i, r):
        if i not in exchanged:
            exchanged.add(i)
            cot_x[i].wait_recv()
        for half in parts(r):
            if half not in gathered:
                gathered.add(half)
                for c in gather[half]:
                    c.wait_recv()
            block = dot(cot_v[:, unit_cols(i)], proj_v[half], ((0,), (0,))).astype(BF16)
            for column in range(NX):
                j, first_row = (column - x + NX) % NX, column * ROWS
                tx[half, i, j] = block[first_row : first_row + RX]
                tz[half, i, j] = block[first_row + RX : first_row + ROWS]

    def x_send(i, r, n, j, k):
        h = r % 2
        send(
            ("x", i, n, r), tx.at[pick(r), i, j % NX], xr.at[pick(r), i, n],
            xr_s.at[h, i, n], xr_r.at[h, i, n], at_x(k),
        )

    def x_open(i, r):
        s = 1 - 2 * (i % 2)
        x_send(i, r, 0, 2, s)
        x_send(i, r, 2, -s, -s)

    def x_forward(i, r):
        s = 1 - 2 * (i % 2)
        need(("x", i, 0), r)
        for half in parts(r):
            tx[half, i, s % NX] = tx[half, i, s % NX] + xr[half, i, 0]
        x_send(i, r, 1, s, s)

    def x_close(i, r):
        s = 1 if STEPS[i] > 0 else -1
        need(("x", i, 1), r)
        need(("x", i, 2), r)
        earlier = {0: (), 1: (0,), 2: (0,), 7: (5, 6)}.get(i, (i - 2,))
        for e in earlier:
            need(("zx", e), r if e else (0 if s == 1 else 1))
        for half in parts(r):
            total = tx[half, i, 0].astype(F32) + xr[half, i, 1].astype(F32) + xr[half, i, 2].astype(F32)
            for e in earlier:
                if e or (half == 0) == (s == 1):
                    total = total + zx[half, e].astype(F32)
            if i == 7:
                adam(total, pl.ds(0, RX), half, 0)
            else:
                tx[half, i, 0] = total.astype(BF16)
        if i == 0:
            for h, k in enumerate((1, -1)):
                send(("zx", 0, h), tx.at[h, 0, 0], zx.at[h, 0], zx_s.at[h, 0], zx_r.at[h, 0], at_z(k))
        elif i < 7:
            h = r % 2
            send(("zx", i, r), tx.at[pick(r), i, 0], zx.at[pick(r), i], zx_s.at[h, i], zx_r.at[h, i], at_z(s))

    def z_step(i, r, g):
        first, count = ((g - 4) * 2, 2) if g > 3 else (g, 1)
        s = 1 if STEPS[i] > 0 else -1
        if i == 0:
            s = 1 if first < 2 else -1
        elif i > 2 or (first < 2) == (s == 1):
            e = max(i - 2, 0)
            for j in range(first, first + count):
                need_z(e, j, r)
                for half in parts(r):
                    tz[half, i, j] = tz[half, i, j] + zz[half, e, j]
        h, blocks = r % 2, pl.ds(first, count)
        send(
            ("z", i, g, r), tz.at[pick(r), i, blocks], zz.at[pick(r), i, blocks],
            zz_s.at[h, i, first], zz_r.at[h, i, first], at_z(s),
        )

    def need_z(e, j, r):
        need(("z", e, j), r)
        need(("z", e, 4 + j // 2), r)

    def z_total(j, half):
        for e in (5, 6):
            need_z(e, j, 2)
        return tz[half, 7, j].astype(F32) + zz[half, 5, j].astype(F32) + zz[half, 6, j].astype(F32)

    def z_open(i, r):
        for h, k in enumerate((1, -1)):
            tz[h, 7, 2] = z_total(2, h).astype(BF16)
            send(("xz", 0, h), tz.at[h, 7, 2], xz.at[h, 0], xz_s.at[h, 0], xz_r.at[h, 0], at_x(k))

    def z_forward(n, i, r):
        s = 1 if n == 1 else -1
        j = s % NX
        need(("xz", 0), 0 if s == 1 else 1)
        for half in range(2):
            total = z_total(j, half)
            if (half == 0) == (s == 1):
                total = total + xz[half, 0].astype(F32)
            tz[half, 7, j] = total.astype(BF16)
        send(("xz", n, 2), tz.at[:, 7, j], xz.at[:, n], xz_s.at[0, n], xz_r.at[0, n], at_x(s))

    def z_close(i, r):
        for n in (1, 2):
            need(("xz", n), 2)
        for half in range(2):
            total = z_total(0, half)
            adam(total + xz[half, 1].astype(F32) + xz[half, 2].astype(F32), pl.ds(RX, RZ), half, 1)


    def adam(lowrank, rows, r, n):
        lanes = pl.ds(r * LANES, LANES)
        for c in get_moments:
            c.wait()
        get_moments.clear()
        fresh_first = beta_first * first_v[rows, lanes] + (1.0 - beta_first) * lowrank
        fresh_second = beta_second * second_v[rows, lanes] + (1.0 - beta_second) * lowrank * lowrank
        new_first[rows, lanes] = fresh_first
        new_second[rows, lanes] = fresh_second
        direction = fresh_first / bias_first / (jnp.sqrt(fresh_second / bias_second) + adam_eps)
        own = pl.ds(pl.multiple_of(core * HALF + r * LANES, LANES), LANES)
        dir_v[rows, own] = direction.astype(BF16)
        send(
            ("dir", n, r), dir_v.at[rows, own], dir_v.at[rows, own], dir_s.at[r, n], dir_r.at[r, n], sibling
        )

    run = {
        "C": compute, "X": x_open, "F": x_forward, "L": x_close,
        "Z": z_step, "O": z_open, "G": z_forward, "H": z_close,
    }
    for name in ORDER:
        run[name[0]](*map(int, name[1:]))
    for n in range(2):
        need(("dir", n), 2)
    assert not pending
    for c in sends:
        c.wait_send()


def back_project(direction, projector, fresh_first, fresh_second, upd, new_first, new_second, upd_v, store):
    stores = [
        pltpu.make_async_copy(fresh_first, new_first.at[0, 0], store.at[0]),
        pltpu.make_async_copy(fresh_second, new_second.at[0, 0], store.at[1]),
    ]
    for c in stores:
        c.start()
    for c in range(WIDTH // COLS):
        part = pl.ds(c * COLS, COLS)
        upd_v[:, part] = dot(direction[...], projector[part, :], ((1,), (1,)))
        stores.append(pltpu.make_async_copy(upd_v.at[:, part], upd.at[0, 0, :, part], store.at[2 + c]))
        stores[-1].start()
    for c in stores:
        c.wait()


def per_device(activations, cotangents, projector, first_moment, second_moment):
    any_space = pl.BlockSpec(memory_space=pl.ANY)
    vmem = pl.BlockSpec(memory_space=pltpu.VMEM)
    dma = pltpu.SemaphoreType.DMA
    direction, fresh_first, fresh_second = pl.pallas_call(
        kernel,
        out_shape=(
            jax.ShapeDtypeStruct((ROWS, RANK), BF16),
            jax.ShapeDtypeStruct((ROWS, HALF), F32),
            jax.ShapeDtypeStruct((ROWS, HALF), F32),
        ),
        in_specs=[any_space] * 5,
        out_specs=(vmem, vmem, vmem),
        scratch_shapes=[
            pltpu.VMEM((TOK, WIDTH), BF16),
            pltpu.VMEM((2, 2, WIDTH, LANES), BF16),
            pltpu.VMEM((512, HID), BF16),
            pltpu.VMEM((2, 2, TOK, LANES), F32),
            pltpu.VMEM((2, TOK, LANES), F32),
            pltpu.VMEM((2, 512, LANES), BF16),
            pltpu.VMEM((2, 8, NX, RX, LANES), BF16),
            pltpu.VMEM((2, 8, NX, RZ, LANES), BF16),
            pltpu.VMEM((2, 8, 3, RX, LANES), BF16),
            pltpu.VMEM((2, 7, NX, RZ, LANES), BF16),
            pltpu.VMEM((2, 7, RX, LANES), BF16),
            pltpu.VMEM((2, 3, RZ, LANES), BF16),
            pltpu.VMEM((ROWS, HALF), F32),
            pltpu.VMEM((ROWS, HALF), F32),
            dma((7,)),
            dma((8,)),
            dma((8,)),
            dma((8,)),
            dma((2,)),
            dma((2,)),
            dma((2, 3)),
            dma((2, 3)),
            dma((2, 8, 3)),
            dma((2, 8, 3)),
            dma((2, 7, NX)),
            dma((2, 7, NX)),
            dma((2, 8)),
            dma((2, 8)),
            dma((2, 4)),
            dma((2, 4)),
            dma((2, 2)),
            dma((2, 2)),
        ],
        compiler_params=pltpu.CompilerParams(
            collective_id=0, has_side_effects=True, vmem_limit_bytes=105 * 2**19
        ),
        name="galore_step",
    )(activations, cotangents, projector, first_moment, second_moment)
    return pl.pallas_call(
        back_project,
        out_shape=(
            jax.ShapeDtypeStruct((1, 1, ROWS, WIDTH), F32),
            jax.ShapeDtypeStruct((1, 1, ROWS, HALF), F32),
            jax.ShapeDtypeStruct((1, 1, ROWS, HALF), F32),
        ),
        in_specs=[vmem] * 4,
        out_specs=(any_space,) * 3,
        scratch_shapes=[pltpu.VMEM((ROWS, WIDTH), F32), dma((2 + WIDTH // COLS,))],
        compiler_params=pltpu.CompilerParams(vmem_limit_bytes=12 * 2**20),
        name="back_project",
    )(direction, projector, fresh_first, fresh_second)


def solution(mesh):
    return jax.shard_map(
        per_device,
        mesh=mesh,
        in_specs=(
            P(None, ("dp", "tensor"), "fsdp"),
            P(None, ("dp", "fsdp"), "tensor"),
            P("fsdp", None),
            P(None, "tensor", "dp", "fsdp"),
            P(None, "tensor", "dp", "fsdp"),
        ),
        out_specs=(
            P(None, "tensor", "dp", "fsdp"),
            P(None, "tensor", "dp", "fsdp"),
            P(None, "tensor", "dp", "fsdp"),
        ),
        check_vma=False,
    )
```

```python
import functools

import jax
import jax.numpy as jnp
from jax import lax
from jax.experimental import pallas as pl
from jax.experimental.pallas import tpu as pltpu
from jax.sharding import PartitionSpec as P

beta_first = 0.9
beta_second = 0.999
bias_first = 1.0 - 0.9**10
bias_second = 1.0 - 0.999**10
adam_eps = 1e-08

NZ, NX, NY = 8, 4, 4
TOK = 128
WIDTH = 4096
RANK = 1024
HALF = 512
ROWS = 224
UNIT = NX * ROWS
HID = NZ * UNIT
RX = 128
RZ = ROWS - RX
LANES = HALF // 2
COLS = 512
F32, BF16 = jnp.float32, jnp.bfloat16
MESH = pl.DeviceIdType.MESH

STEPS = (4, 3, -3, 2, -2, 1, -1, 0)

ORDER = (
    "C00", "Z004", "X00", "Z005", "C10", "X10", "Z105", "C20", "C01", "Z015", "X01", "X20", "Z204", "C30",
    "Z014", "C11", "Z115", "X11", "C41", "C40", "Z205", "C21", "X21", "Z104", "F02", "X30", "C31", "Z215",
    "X31", "C62", "Z114", "Z305", "X42", "C72", "Z404", "F12", "X62", "C52", "Z315", "F22", "Z214", "Z405",
    "X72", "X52", "Z304", "Z415", "L02", "F32", "Z314", "Z414", "Z523", "Z522", "F40", "F41", "Z623", "Z622",
    "F60", "F61", "L12", "Z521", "Z520", "L22", "F70", "Z621", "Z620", "F71", "F50", "F51", "O72", "L30",
    "L31", "L40", "L41", "L50", "G172", "G272", "L60", "L51", "L61", "L70", "H72", "L71",
)


def dot(a, b, dims):
    return lax.dot_general(a, b, (dims, ((), ())), preferred_element_type=F32)


def kernel(
    act, cot, projector, first, second, dir_v, new_first, new_second,
    act_v, prj_v, cot_v, part_v, other_v, proj_v, tx, tz, xr, zz, zx, xz, first_v, second_v,
    load, cot_load, cot_s, cot_r, part_s, part_r, y_s, y_r, xr_s, xr_r, zz_s, zz_r,
    zx_s, zx_r, xz_s, xz_r, dir_s, dir_r,
):
    dp, core, y = lax.axis_index("dp"), lax.axis_index("fsdp"), lax.axis_index("tensor")
    z, x = dp // NX, dp % NX

    def at_x(k):
        return (z * NX + (x + k + NX) % NX, core, y)

    def at_z(k):
        return (((z + k + NZ) % NZ) * NX + x, core, y)

    def at_y(k):
        return (dp, core, (y + k) % NY)

    sibling = (dp, 1 - core, y)

    def remote(src, dst, send, recv, device):
        return pltpu.make_async_remote_copy(
            src_ref=src, dst_ref=dst, send_sem=send, recv_sem=recv, device_id=device, device_id_type=MESH
        )

    barrier = pltpu.get_barrier_semaphore()
    for device in (sibling, at_y(1), at_y(2), at_y(3), at_x(1), at_x(-1), at_z(1), at_z(-1)):
        pl.semaphore_signal(barrier, inc=1, device_id=device, device_id_type=MESH)

    def unit_cols(i):
        return pl.ds(pl.multiple_of(((z + STEPS[i] + NZ) % NZ) * UNIT, UNIT), UNIT)

    own_tok = pl.ds(pl.multiple_of(core * 256, 256), 256)
    get_act = pltpu.make_async_copy(act.at[0], act_v, load.at[0])
    get_act.start()
    get_prj = []
    for r in range(2):
        for h in range(2):
            share = core if h else 1 - core
            cols = pl.ds(pl.multiple_of(share * HALF + r * LANES, LANES), LANES)
            get_prj.append(pltpu.make_async_copy(projector.at[:, cols], prj_v.at[r, h], load.at[1 + 2 * r + h]))
            if r == 0:
                get_prj[-1].start()
    get_moments = [
        pltpu.make_async_copy(first.at[0, 0], first_v, load.at[5]),
        pltpu.make_async_copy(second.at[0, 0], second_v, load.at[6]),
    ]
    cot_in = [
        pltpu.make_async_copy(cot.at[0, :, unit_cols(i)], cot_v.at[own_tok, unit_cols(i)], cot_load.at[i])
        for i in range(NZ)
    ]
    cot_x = [
        remote(
            cot_v.at[own_tok, unit_cols(i)], cot_v.at[own_tok, unit_cols(i)], cot_s.at[i], cot_r.at[i], sibling
        )
        for i in range(NZ)
    ]

    pl.semaphore_wait(barrier, 8)

    swap = [
        remote(part_v.at[r, 1 - core], other_v.at[r], part_s.at[r], part_r.at[r], sibling) for r in range(2)
    ]
    own_rows = pl.ds(pl.multiple_of(y * TOK, TOK), TOK)
    gather = [
        [
            remote(proj_v.at[r, own_rows], proj_v.at[r, own_rows], y_s.at[r, k - 1], y_r.at[r, k - 1], at_y(k))
            for k in (2, 1, 3)
        ]
        for r in range(2)
    ]
    get_act.wait()
    for r in range(2):
        get_prj[2 * r].wait()
        part_v[r, 1 - core] = dot(act_v[...], prj_v[r, 0], ((1,), (0,)))
        swap[r].start()
        get_prj[2 * r + 1].wait()
        for c in (get_prj[2:] if r == 0 else cot_in + get_moments):
            c.start()
        part_v[r, core] = dot(act_v[...], prj_v[r, 1], ((1,), (0,)))
        swap[r].wait_recv()
        proj_v[r, own_rows, :] = (part_v[r, core] + other_v[r]).astype(BF16)
        for c in gather[r]:
            c.start()
    for i in range(NZ):
        cot_in[i].wait()
        cot_x[i].start()

    sends = cot_x + swap + gather[0] + gather[1]
    pending = {}

    def send(key, src, dst, send_sem, recv_sem, device):
        copy = remote(src, dst, send_sem, recv_sem, device)
        copy.start()
        sends.append(copy)
        pending[key] = copy

    def parts(r):
        return (0, 1) if r == 2 else (r,)

    def pick(r):
        return slice(None) if r == 2 else r

    def need(kind, r):
        for half in parts(r) + (2,):
            copy = pending.pop(kind + (half,), None)
            if copy is not None:
                copy.wait_recv()

    gathered, exchanged = set(), set()

    def compute(i, r):
        if i not in exchanged:
            exchanged.add(i)
            cot_x[i].wait_recv()
        for half in parts(r):
            if half not in gathered:
                gathered.add(half)
                for c in gather[half]:
                    c.wait_recv()
            block = dot(cot_v[:, unit_cols(i)], proj_v[half], ((0,), (0,))).astype(BF16)
            for column in range(NX):
                j, first_row = (column - x + NX) % NX, column * ROWS
                tx[half, i, j] = block[first_row : first_row + RX]
                tz[half, i, j] = block[first_row + RX : first_row + ROWS]

    def x_send(i, r, n, j, k):
        h = r % 2
        send(
            ("x", i, n, r), tx.at[pick(r), i, j % NX], xr.at[pick(r), i, n],
            xr_s.at[h, i, n], xr_r.at[h, i, n], at_x(k),
        )

    def x_open(i, r):
        s = 1 - 2 * (i % 2)
        x_send(i, r, 0, 2, s)
        x_send(i, r, 2, -s, -s)

    def x_forward(i, r):
        s = 1 - 2 * (i % 2)
        need(("x", i, 0), r)
        for half in parts(r):
            tx[half, i, s % NX] = tx[half, i, s % NX] + xr[half, i, 0]
        x_send(i, r, 1, s, s)

    def x_close(i, r):
        s = 1 if STEPS[i] > 0 else -1
        need(("x", i, 1), r)
        need(("x", i, 2), r)
        earlier = {0: (), 1: (0,), 2: (0,), 7: (5, 6)}.get(i, (i - 2,))
        for e in earlier:
            need(("zx", e), r if e else (0 if s == 1 else 1))
        for half in parts(r):
            total = tx[half, i, 0].astype(F32) + xr[half, i, 1].astype(F32) + xr[half, i, 2].astype(F32)
            for e in earlier:
                if e or (half == 0) == (s == 1):
                    total = total + zx[half, e].astype(F32)
            if i == 7:
                adam(total, pl.ds(0, RX), half, 0)
            else:
                tx[half, i, 0] = total.astype(BF16)
        if i == 0:
            for h, k in enumerate((1, -1)):
                send(("zx", 0, h), tx.at[h, 0, 0], zx.at[h, 0], zx_s.at[h, 0], zx_r.at[h, 0], at_z(k))
        elif i < 7:
            h = r % 2
            send(("zx", i, r), tx.at[pick(r), i, 0], zx.at[pick(r), i], zx_s.at[h, i], zx_r.at[h, i], at_z(s))

    def z_step(i, r, g):
        first, count = ((g - 4) * 2, 2) if g > 3 else (g, 1)
        s = 1 if STEPS[i] > 0 else -1
        if i == 0:
            s = 1 if first < 2 else -1
        elif i > 2 or (first < 2) == (s == 1):
            e = max(i - 2, 0)
            for j in range(first, first + count):
                need_z(e, j, r)
                for half in parts(r):
                    tz[half, i, j] = tz[half, i, j] + zz[half, e, j]
        h, blocks = r % 2, pl.ds(first, count)
        send(
            ("z", i, g, r), tz.at[pick(r), i, blocks], zz.at[pick(r), i, blocks],
            zz_s.at[h, i, first], zz_r.at[h, i, first], at_z(s),
        )

    def need_z(e, j, r):
        need(("z", e, j), r)
        need(("z", e, 4 + j // 2), r)

    def z_total(j, half):
        for e in (5, 6):
            need_z(e, j, 2)
        return tz[half, 7, j].astype(F32) + zz[half, 5, j].astype(F32) + zz[half, 6, j].astype(F32)

    def z_open(i, r):
        for h, k in enumerate((1, -1)):
            tz[h, 7, 2] = z_total(2, h).astype(BF16)
            send(("xz", 0, h), tz.at[h, 7, 2], xz.at[h, 0], xz_s.at[h, 0], xz_r.at[h, 0], at_x(k))

    def z_forward(n, i, r):
        s = 1 if n == 1 else -1
        j = s % NX
        need(("xz", 0), 0 if s == 1 else 1)
        for half in range(2):
            total = z_total(j, half)
            if (half == 0) == (s == 1):
                total = total + xz[half, 0].astype(F32)
            tz[half, 7, j] = total.astype(BF16)
        send(("xz", n, 2), tz.at[:, 7, j], xz.at[:, n], xz_s.at[0, n], xz_r.at[0, n], at_x(s))

    def z_close(i, r):
        for n in (1, 2):
            need(("xz", n), 2)
        for half in range(2):
            total = z_total(0, half)
            adam(total + xz[half, 1].astype(F32) + xz[half, 2].astype(F32), pl.ds(RX, RZ), half, 1)


    def adam(lowrank, rows, r, n):
        lanes = pl.ds(r * LANES, LANES)
        for c in get_moments:
            c.wait()
        get_moments.clear()
        fresh_first = beta_first * first_v[rows, lanes] + (1.0 - beta_first) * lowrank
        fresh_second = beta_second * second_v[rows, lanes] + (1.0 - beta_second) * lowrank * lowrank
        new_first[rows, lanes] = fresh_first
        new_second[rows, lanes] = fresh_second
        direction = fresh_first / bias_first / (jnp.sqrt(fresh_second / bias_second) + adam_eps)
        own = pl.ds(pl.multiple_of(core * HALF + r * LANES, LANES), LANES)
        dir_v[rows, own] = direction.astype(BF16)
        send(
            ("dir", n, r), dir_v.at[rows, own], dir_v.at[rows, own], dir_s.at[r, n], dir_r.at[r, n], sibling
        )

    run = {
        "C": compute, "X": x_open, "F": x_forward, "L": x_close,
        "Z": z_step, "O": z_open, "G": z_forward, "H": z_close,
    }
    for name in ORDER:
        run[name[0]](*map(int, name[1:]))
    for n in range(2):
        need(("dir", n), 2)
    assert not pending
    for c in sends:
        c.wait_send()


def back_project(direction, projector, fresh_first, fresh_second, upd, new_first, new_second, upd_v, store):
    stores = [
        pltpu.make_async_copy(fresh_first, new_first.at[0, 0], store.at[0]),
        pltpu.make_async_copy(fresh_second, new_second.at[0, 0], store.at[1]),
    ]
    for c in stores:
        c.start()
    for c in range(WIDTH // COLS):
        part = pl.ds(c * COLS, COLS)
        upd_v[:, part] = dot(direction[...], projector[part, :], ((1,), (1,)))
        stores.append(pltpu.make_async_copy(upd_v.at[:, part], upd.at[0, 0, :, part], store.at[2 + c]))
        stores[-1].start()
    for c in stores:
        c.wait()


def per_device(activations, cotangents, projector, first_moment, second_moment):
    any_space = pl.BlockSpec(memory_space=pl.ANY)
    vmem = pl.BlockSpec(memory_space=pltpu.VMEM)
    dma = pltpu.SemaphoreType.DMA
    direction, fresh_first, fresh_second = pl.pallas_call(
        kernel,
        out_shape=(
            jax.ShapeDtypeStruct((ROWS, RANK), BF16),
            jax.ShapeDtypeStruct((ROWS, HALF), F32),
            jax.ShapeDtypeStruct((ROWS, HALF), F32),
        ),
        in_specs=[any_space] * 5,
        out_specs=(vmem, vmem, vmem),
        scratch_shapes=[
            pltpu.VMEM((TOK, WIDTH), BF16),
            pltpu.VMEM((2, 2, WIDTH, LANES), BF16),
            pltpu.VMEM((512, HID), BF16),
            pltpu.VMEM((2, 2, TOK, LANES), F32),
            pltpu.VMEM((2, TOK, LANES), F32),
            pltpu.VMEM((2, 512, LANES), BF16),
            pltpu.VMEM((2, 8, NX, RX, LANES), BF16),
            pltpu.VMEM((2, 8, NX, RZ, LANES), BF16),
            pltpu.VMEM((2, 8, 3, RX, LANES), BF16),
            pltpu.VMEM((2, 7, NX, RZ, LANES), BF16),
            pltpu.VMEM((2, 7, RX, LANES), BF16),
            pltpu.VMEM((2, 3, RZ, LANES), BF16),
            pltpu.VMEM((ROWS, HALF), F32),
            pltpu.VMEM((ROWS, HALF), F32),
            dma((7,)),
            dma((8,)),
            dma((8,)),
            dma((8,)),
            dma((2,)),
            dma((2,)),
            dma((2, 3)),
            dma((2, 3)),
            dma((2, 8, 3)),
            dma((2, 8, 3)),
            dma((2, 7, NX)),
            dma((2, 7, NX)),
            dma((2, 8)),
            dma((2, 8)),
            dma((2, 4)),
            dma((2, 4)),
            dma((2, 2)),
            dma((2, 2)),
        ],
        compiler_params=pltpu.CompilerParams(
            collective_id=0, has_side_effects=True, vmem_limit_bytes=105 * 2**19
        ),
        name="galore_step",
    )(activations, cotangents, projector, first_moment, second_moment)
    return pl.pallas_call(
        back_project,
        out_shape=(
            jax.ShapeDtypeStruct((1, 1, ROWS, WIDTH), F32),
            jax.ShapeDtypeStruct((1, 1, ROWS, HALF), F32),
            jax.ShapeDtypeStruct((1, 1, ROWS, HALF), F32),
        ),
        in_specs=[vmem] * 4,
        out_specs=(any_space,) * 3,
        scratch_shapes=[pltpu.VMEM((ROWS, WIDTH), F32), dma((2 + WIDTH // COLS,))],
        compiler_params=pltpu.CompilerParams(vmem_limit_bytes=12 * 2**20),
        name="back_project",
    )(direction, projector, fresh_first, fresh_second)


def solution(mesh):
    return jax.shard_map(
        per_device,
        mesh=mesh,
        in_specs=(
            P(None, ("dp", "tensor"), "fsdp"),
            P(None, ("dp", "fsdp"), "tensor"),
            P("fsdp", None),
            P(None, "tensor", "dp", "fsdp"),
            P(None, "tensor", "dp", "fsdp"),
        ),
        out_specs=(
            P(None, "tensor", "dp", "fsdp"),
            P(None, "tensor", "dp", "fsdp"),
            P(None, "tensor", "dp", "fsdp"),
        ),
        check_vma=False,
    )
```
